32 devices in a mesh: dp: 8 (over y, x, core), mp: 4 (over z).
Axes of the slice: x: 2, y: 2, z: 4, core: 2. Of those that a mesh axis runs over, the one named last changes fastest.
Arguments:
- pooled: bfloat16 [4096, 512], P('dp', 'mp')
- delta: bfloat16 [4096, 2048], P('dp')
- w_first: bfloat16 [512, 2048], P('mp'), may hold values from -0.25 to 0.25
- lookup_slot: int32 [4096, 4, 8], P('dp', 'mp'), may hold values from 0 to 1023, as said below
- row_ids: int32 [8, 4, 1024], P('dp', 'mp'), may hold values from 0 to 511, as said below
- send_counts: int32 [8, 4, 4], P('dp', 'mp'), may hold values from 32 to 256, as said below
Outputs:
- dense_grad: float32 [512, 2048], P('mp')
- table_grad: float32 [8, 4, 2048, 128], P('dp', None, 'mp')
The draws below stay inside these ranges and needn't reach their ends.
Inputs may be any that keep to these rules, and one draw needn't show every extreme that they name: `lookup_slot`: within one block (d, t), every entry k below the sum of send_counts[d, t, :] is named by at least one lookup of that block's examples, and no lookup names a larger entry. `row_ids`: within one block and one owner's entries the row numbers are distinct; entries past the block's total are 0. `send_counts`: in every block (d, t) some owner gets exactly 256 entries.
All inputs are finite; a program needn't handle non-finite values.
Results may differ from the reference program's by a relative error of at most 0.0028.
Values sent between devices are 32-bit elements; how exact they have to be, the bound alone decides.
No kernel may reach another device: no remote copies, remote signals or barrier semaphores. Data moves between devices by JAX's collectives and lax.ppermute only.
A program may use at most 64 MiB of HBM per device.

```python
import math
import jax
import jax.numpy as jnp
from jax import lax

EMB = 128
HID = 2048
LOOK = 8
CAP = 256
B_DEV = 512
ROWS_DEV = 512
NTAB = 4
EXAMPLES = 4096
N_DP = 8
N_MP = 4


def layout(key):
    blocks = N_DP * NTAB
    width = N_MP * CAP
    key_hot, key_counts, key_ids, key_fill, key_order = jax.random.split(key, 5)
    hot = jax.random.randint(key_hot, (blocks, 1), 0, N_MP)
    least = max(CAP // 8, 1)
    light = jax.random.randint(key_counts, (blocks, N_MP), least, CAP // 2 + 1)
    block_index = jnp.arange(blocks, dtype=jnp.int32)[:, None]
    light = jnp.where(block_index == 1, least, light)
    counts = jnp.where(jnp.arange(N_MP, dtype=jnp.int32)[None, :] == hot, CAP, light)
    counts = jnp.where(block_index == 0, CAP, counts).astype(jnp.int32)
    perm_keys = jax.random.split(key_ids, blocks * N_MP)
    chosen = jax.vmap(lambda k: jnp.concatenate([jax.random.permutation(k, ROWS_DEV - 1)[:CAP - 1], jnp.full((1,), ROWS_DEV - 1, jnp.int32)]))(perm_keys).reshape(blocks, N_MP, CAP)
    ends = jnp.cumsum(counts, axis=1)
    starts = ends - counts
    place = jnp.arange(width, dtype=jnp.int32)
    owner = jnp.sum((place[None, :, None] >= ends[:, None, :]).astype(jnp.int32), axis=2)
    total = ends[:, -1:]
    inside = place[None, :] < total
    owner_kept = jnp.minimum(owner, N_MP - 1)
    offset = jnp.clip(place[None, :] - jnp.take_along_axis(starts, owner_kept, axis=1), 0, CAP - 1)
    ids = jnp.where(inside, chosen[jnp.arange(blocks)[:, None], owner_kept, offset], 0)
    lookups = B_DEV * LOOK
    rank = jnp.arange(lookups, dtype=jnp.int32)
    extra = jax.random.randint(key_fill, (blocks, lookups), 0, total)
    base = jnp.where(rank[None, :] < total, rank[None, :], extra)
    order = jax.vmap(lambda k: jax.random.permutation(k, lookups))(jax.random.split(key_order, blocks))
    slots = jnp.take_along_axis(base, order, axis=1)
    slots = jnp.transpose(slots.reshape(N_DP, NTAB, B_DEV, LOOK), (0, 2, 1, 3)).reshape(EXAMPLES, NTAB, LOOK)
    return (slots.astype(jnp.int32), ids.reshape(N_DP, NTAB, width).astype(jnp.int32), counts.reshape(N_DP, NTAB, N_MP))


def draw_lookup_slot(key, part):
    return layout(key)[0]


def draw_row_ids(key, part):
    return layout(key)[1]


def draw_send_counts(key, part):
    return layout(key)[2]


def draw_delta(key, part):
    key = jax.random.fold_in(key, 11)
    key_rows, key_vals = jax.random.split(key, 2)
    scales = jnp.exp(jax.random.uniform(key_rows, (EXAMPLES, 1), minval=math.log(0.005), maxval=math.log(0.5)))
    values = jax.random.normal(key_vals, (EXAMPLES, HID))
    return (values * scales).astype(jnp.bfloat16)


def draw_pooled(key, part):
    key = jax.random.fold_in(key, 12)
    key_vals = jax.random.fold_in(key, 0)
    column = jnp.arange(NTAB * EMB, dtype=jnp.int32) // EMB
    factor = 1.0 + 3.0 * column.astype(jnp.float32) / (NTAB - 1)
    values = jax.random.normal(key_vals, (EXAMPLES, NTAB * EMB))
    return (0.037 * values * factor[None, :]).astype(jnp.bfloat16)


def shard_levels(key, shape, cuts, smallest, top_value):
    factor_of, own = 1.0, jax.random.fold_in(key, 6)
    for axis_at, parts in cuts:
        steps = jnp.exp(jax.random.uniform(jax.random.fold_in(own, axis_at), (parts,), jnp.float32, smallest / len(cuts), top_value / len(cuts)))
        factor_of = factor_of * jnp.repeat(steps, shape[axis_at] // parts).reshape([-1 if axis == axis_at else 1 for axis in range(len(shape))])
    return factor_of


def centred(own_key, extent, deviation, bound, pieces=(), kind=jnp.bfloat16):
    loudness = shard_levels(own_key, extent, pieces, -0.22, 0.18) if pieces else 1.0
    array = jax.random.normal(own_key, extent, jnp.float32) * deviation * loudness
    return jnp.minimum(jnp.maximum(array, -bound), bound).astype(kind)


def setup_inputs(seed: int = 0) -> dict:
    splits = jax.random.split(jax.random.key(seed), 7)
    return {
        "pooled": draw_pooled(jax.random.fold_in(splits[6], 71), 0),
        "delta": draw_delta(jax.random.fold_in(splits[6], 71), 0),
        "w_first": centred(splits[2], (NTAB * EMB, HID), (NTAB * EMB) ** -0.5, 0.25, ((0, 4),)),
        "lookup_slot": draw_lookup_slot(jax.random.fold_in(splits[6], 71), 0),
        "row_ids": draw_row_ids(jax.random.fold_in(splits[6], 71), 0),
        "send_counts": draw_send_counts(jax.random.fold_in(splits[6], 71), 0),
    }


CLIP_NORM = 8.0
EPSILON = 1e-06

def block_rows(contrib_block, slot_block, ids_block, counts_block):
    width = ids_block.shape[1]

    def one_table(items):
        values, slots, ids, counts = items
        unique = jax.ops.segment_sum(jnp.repeat(values, LOOK, axis=0), slots.reshape(-1), num_segments=width)
        ends = jnp.cumsum(counts)
        place = jnp.arange(width, dtype=jnp.int32)
        owner = lax.optimization_barrier(jnp.sum((place[:, None] >= ends[None, :]).astype(jnp.int32), axis=1))
        valid = owner < N_MP
        target = jnp.where(valid, jnp.minimum(owner, N_MP - 1) * ROWS_DEV + ids, 0).astype(jnp.int32)
        start = jnp.zeros((ROWS_DEV * N_MP, EMB), jnp.float32)
        return start.at[target].add(jnp.where(valid[:, None], unique, 0.0))
    return lax.map(one_table, (jnp.transpose(contrib_block, (1, 0, 2)), jnp.transpose(slot_block, (1, 0, 2)), ids_block, counts_block))

def reference(pooled, delta, w_first, lookup_slot, row_ids, send_counts):
    xgrad = jnp.dot(delta, w_first.T, preferred_element_type=jnp.float32)
    grouped = xgrad.reshape(EXAMPLES, NTAB, EMB)
    repeats = lax.optimization_barrier(jnp.sum((lookup_slot[:, :, :, None] == lookup_slot[:, :, None, :]).astype(jnp.float32), axis=(2, 3)))
    embed_sq = lax.optimization_barrier(jnp.sum(repeats * lax.optimization_barrier(jnp.sum(grouped * grouped, axis=2)), axis=1))
    pooled_wide = pooled.astype(jnp.float32)
    delta_wide = delta.astype(jnp.float32)
    norm_sq = lax.optimization_barrier(jnp.sum(delta_wide * delta_wide, axis=1)) * lax.optimization_barrier(jnp.sum(pooled_wide * pooled_wide, axis=1)) + embed_sq
    clip = jnp.minimum(1.0, CLIP_NORM / jnp.sqrt(norm_sq + EPSILON))
    scaled = (pooled_wide * clip[:, None]).astype(jnp.bfloat16)
    dense_grad = jnp.dot(scaled.T, delta, preferred_element_type=jnp.float32)
    contrib = (grouped * clip[:, None, None]).reshape(N_DP, B_DEV, NTAB, EMB)
    slots = lookup_slot.reshape(N_DP, B_DEV, NTAB, LOOK)
    table_grad = lax.map(lambda items: block_rows(items[0], items[1], items[2], items[3]), (contrib, slots, row_ids, send_counts))
    return (dense_grad, table_grad)
```

```python
import jax
import jax.numpy as jnp
from jax import lax
from jax.sharding import PartitionSpec as P

ROWS_DEV = 512
CLIP_NORM = 8.0
EPSILON = 1e-06


def peers(n):
    if n & (n - 1) == 0:
        return [[(i, i ^ s) for i in range(n)] for s in range(1, n)]
    return [[(i, (i + s) % n) for i in range(n)] for s in range(1, n)]


def peer_to(me, s, n):
    return me ^ s if n & (n - 1) == 0 else lax.rem(me + s, n)


def peer_from(me, s, n):
    return me ^ s if n & (n - 1) == 0 else lax.rem(me + n - s, n)


def split(x):
    hi = lax.reduce_precision(x, 8, 7)
    return hi.astype(jnp.bfloat16), (x - hi).astype(jnp.bfloat16)


def dense_sum(local, n_dp):
    if n_dp != 8:
        return lax.psum(local, "dp")
    rows = local.shape[0]
    half, part = rows // 2, rows // 8
    me = lax.axis_index("dp")
    core, chip = me & 1, me >> 1
    swap = [(i, i ^ 1) for i in range(8)]
    theirs = lax.dynamic_slice_in_dim(local, (1 - core) * half, half, 0)
    mine = lax.dynamic_slice_in_dim(local, core * half, half, 0)
    mine = mine + lax.ppermute(theirs, "dp", swap)
    total = lax.dynamic_slice_in_dim(mine, chip * part, part, 0)
    got = []
    for s in (1, 2, 3):
        piece = lax.dynamic_slice_in_dim(mine, (chip ^ s) * part, part, 0)
        got.append(lax.ppermute(piece, "dp", [(i, i ^ (2 * s)) for i in range(8)]))
    total = total + got[0] + got[1] + got[2]
    own = jnp.zeros((half, local.shape[1]), jnp.float32)
    own = lax.dynamic_update_slice_in_dim(own, total, chip * part, 0)
    for s in (1, 2, 3):
        piece = lax.ppermute(total, "dp", [(i, i ^ (2 * s)) for i in range(8)])
        own = lax.dynamic_update_slice_in_dim(own, piece, (chip ^ s) * part, 0)
    other = lax.ppermute(own, "dp", swap)
    out = jnp.zeros(local.shape, jnp.float32)
    out = lax.dynamic_update_slice_in_dim(out, own, core * half, 0)
    return lax.dynamic_update_slice_in_dim(out, other, (1 - core) * half, 0)


def on_device(pooled, delta, w_first, lookup_slot, row_ids, send_counts):
    owners = lax.axis_size("mp")
    n_dp = lax.axis_size("dp")
    me = lax.axis_index("mp")
    width = row_ids.shape[-1]
    cap = width // owners
    xgrad = lax.dot_general(
        w_first, delta, (((1,), (1,)), ((), ())), preferred_element_type=jnp.float32
    )
    slots = lookup_slot[:, 0, :].T
    looks = slots.shape[0]
    pairs = jnp.zeros(slots.shape[1:], jnp.float32)
    for a in range(looks):
        for b in range(a):
            pairs = pairs + (slots[a] == slots[b]).astype(jnp.float32)
    repeats = looks + 2.0 * pairs
    pooled_t = pooled.astype(jnp.float32).T
    delta_wide = delta.astype(jnp.float32)
    partial = jnp.sum(delta_wide * delta_wide, axis=1) * jnp.sum(pooled_t * pooled_t, axis=0)
    partial = partial + repeats * jnp.sum(xgrad * xgrad, axis=0)

    counts = send_counts[0, 0]
    order = jnp.arange(owners, dtype=jnp.int32)
    ids = jnp.pad(row_ids[0, 0], (0, cap))
    place = jnp.arange(cap, dtype=jnp.int32)
    names, targets = [], []
    for s in range(owners):
        owner = peer_to(me, s, owners)
        start = jnp.sum(jnp.where(order < owner, counts, 0))
        count = jnp.sum(jnp.where(order == owner, counts, 0))
        names.append(jnp.where(place < count, start + place, -1))
        targets.append(jnp.where(place < count, lax.dynamic_slice_in_dim(ids, start, cap, 0), -1))
    perms = peers(owners)
    norm_sq, rows = partial, [targets[0]]
    arrived = []
    for s in range(1, owners):
        message = jnp.concatenate([partial, targets[s].astype(jnp.float32)])
        arrived.append(lax.ppermute(message, "mp", perms[s - 1]))
    for message in arrived:
        norm_sq = norm_sq + message[: partial.shape[0]]
        rows.append(message[partial.shape[0]:].astype(jnp.int32))
    names = jnp.concatenate(names)
    named = jnp.zeros((width, slots.shape[1]), jnp.float32)
    for a in range(looks):
        named = named + (slots[a][None, :] == names[:, None]).astype(jnp.float32)
    named = named.astype(jnp.bfloat16)

    clip = jnp.minimum(1.0, CLIP_NORM / jnp.sqrt(norm_sq + EPSILON))
    scaled = (pooled_t * clip[None, :]).astype(jnp.bfloat16)
    local_dense = jnp.dot(scaled, delta, preferred_element_type=jnp.float32)
    hi, lo = split(xgrad * clip[None, :])
    both = lax.dot_general(
        named, jnp.concatenate([hi, lo]), (((1,), (1,)), ((), ())),
        preferred_element_type=jnp.float32,
    )
    emb = hi.shape[0]
    unique = both[:, :emb] + both[:, emb:]
    dense_grad = dense_sum(local_dense, n_dp)

    received = [unique[:cap]]
    for s in range(1, owners):
        received.append(lax.ppermute(unique[s * cap:(s + 1) * cap], "mp", perms[s - 1]))
    row = jnp.arange(ROWS_DEV, dtype=jnp.int32)
    table_grad = jnp.zeros((owners, ROWS_DEV, emb), jnp.float32)
    for s in range(owners):
        hi, lo = split(received[s])
        hot = (row[:, None] == rows[s][None, :]).astype(jnp.bfloat16)
        placed = jnp.dot(hot, jnp.concatenate([hi, lo], axis=1), preferred_element_type=jnp.float32)
        placed = placed[:, :emb] + placed[:, emb:]
        table_grad = lax.dynamic_update_slice_in_dim(
            table_grad, placed[None], peer_from(me, s, owners), 0
        )
    return (dense_grad, table_grad[None])


def solution(mesh):
    placed = (
        P("dp", "mp"),
        P("dp", None),
        P("mp", None),
        P("dp", "mp", None),
        P("dp", "mp", None),
        P("dp", "mp", None),
    )
    return jax.shard_map(
        on_device,
        mesh=mesh,
        in_specs=placed,
        out_specs=(P("mp", None), P("dp", None, "mp", None)),
        check_vma=False,
    )
```

```python
import functools

import jax
import jax.numpy as jnp
from jax import lax
from jax.experimental import pallas as pl
from jax.experimental.pallas import tpu as pltpu
from jax.sharding import PartitionSpec as P

ROWS_DEV = 512
CLIP_NORM = 8.0
EPSILON = 1e-06

VMEM = pl.BlockSpec(memory_space=pltpu.VMEM)
SMEM = pl.BlockSpec(memory_space=pltpu.SMEM)
HBM = pl.BlockSpec(memory_space=pltpu.HBM)
ANY = pl.BlockSpec(memory_space=pl.ANY)
CHUNK = 256
F32, BF16, I32 = jnp.float32, jnp.bfloat16, jnp.int32


def pairings(n):
    if n & (n - 1) == 0:
        return [[(i, i ^ s) for i in range(n)] for s in range(1, n)]
    return [[(i, (i + s) % n) for i in range(n)] for s in range(1, n)]


def peer_to(me, s, n):
    return me ^ s if n & (n - 1) == 0 else lax.rem(me + s, n)


def peer_from(me, s, n):
    return me ^ s if n & (n - 1) == 0 else lax.rem(me + n - s, n)


def call(kernel, outs, flops, *args, specs=None, out_specs=None, scratch=(), aliases=None):
    size = sum(a.size * a.dtype.itemsize for a in args)
    return list(pl.pallas_call(
        kernel,
        out_shape=[jax.ShapeDtypeStruct(shape, dtype) for shape, dtype in outs],
        in_specs=specs or [VMEM] * len(args),
        out_specs=out_specs or [VMEM] * len(outs),
        scratch_shapes=list(scratch),
        input_output_aliases=aliases or {},
        compiler_params=pltpu.CompilerParams(vmem_limit_bytes=16 * 2**20),
        cost_estimate=pl.CostEstimate(flops=flops, bytes_accessed=size, transcendentals=0),
    )(*args))


def window(counts_ref, me, s, owners):
    owner = peer_to(me, s, owners)
    start, count = jnp.int32(0), jnp.int32(0)
    for o in range(owners):
        here = counts_ref[0, o]
        start = start + jnp.where(o < owner, here, 0)
        count = count + jnp.where(o == owner, here, 0)
    return start, count


def first_kernel(owners, counts_hbm, delta_hbm, w_hbm, pooled_hbm, slots_hbm, ids_hbm, *refs):
    xgrad_ref, delta_ref, pooled_ref, slots_ref, *rest = refs
    message_refs, (w_ref, ids_ref, counts_ref, sems) = rest[:owners], rest[owners:]
    examples, emb = pooled_ref.shape
    hid = delta_ref.shape[1]
    looks = slots_ref.shape[0]
    width = ids_ref.shape[1]
    cap = width // owners
    blocks = list(range(0, examples, CHUNK))
    pairs = [(w_hbm, w_ref)]
    pairs += [(delta_hbm.at[pl.ds(r, CHUNK)], delta_ref.at[pl.ds(r, CHUNK)]) for r in blocks]
    pairs += [(counts_hbm, counts_ref), (slots_hbm, slots_ref), (ids_hbm, ids_ref), (pooled_hbm, pooled_ref)]
    copies = [pltpu.make_async_copy(a, b, sems.at[i]) for i, (a, b) in enumerate(pairs)]
    for copy in copies:
        copy.start()
    me = lax.axis_index("mp")
    n = len(blocks)
    copies[0].wait()
    norms = []
    for i, r in enumerate(blocks):
        copies[1 + i].wait()
        xgrad = lax.dot_general(
            w_ref[...], delta_ref[r:r + CHUNK, :], (((1,), (1,)), ((), ())),
            preferred_element_type=F32,
        )
        xgrad_ref[:, r:r + CHUNK] = xgrad
        sums = []
        for q in range(r, r + CHUNK, 128):
            total = jnp.zeros((128, 128), F32)
            for c in range(0, hid, 128):
                piece = delta_ref[q:q + 128, c:c + 128].astype(F32)
                total = total + piece * piece
            sums.append(jnp.sum(total.T, axis=0, keepdims=True))
        norms.append((jnp.sum(xgrad * xgrad, axis=0, keepdims=True), jnp.concatenate(sums, axis=1)))
    for copy in copies[1 + n:]:
        copy.wait()
    slots = slots_ref[...]
    same = jnp.full(slots.shape, 1.0, F32)
    for shift in range(1, looks):
        same = same + jnp.where(slots == pltpu.roll(slots, shift, 0), 1.0, 0.0)
    repeats = jnp.sum(same, axis=0, keepdims=True)
    for i, r in enumerate(blocks):
        xgrad_sq, delta_sq = norms[i]
        sums = []
        for q in range(r, r + CHUNK, 128):
            piece = pooled_ref[q:q + 128, :].astype(F32)
            sums.append(jnp.sum((piece * piece).T, axis=0, keepdims=True))
        partial = delta_sq * jnp.concatenate(sums, axis=1) + repeats[:, r:r + CHUNK] * xgrad_sq
        for message in message_refs:
            message[:, r:r + CHUNK] = partial
    ids = jnp.broadcast_to(ids_ref[...], (8, width))
    place = lax.broadcasted_iota(I32, (1, cap), 1)
    for s in range(owners):
        start, count = window(counts_ref, me, s, owners)
        mine = pltpu.roll(ids, lax.rem(width - start, width), 1)[0:1, :cap]
        message_refs[s][:, examples:] = jnp.where(place < count, mine, -1).astype(F32)


def named_kernel(owners, counts_ref, slots_ref, named_ref):
    width = named_ref.shape[0]
    looks, examples = slots_ref.shape
    cap = width // owners
    me = lax.axis_index("mp")
    for s in range(owners):
        start, count = window(counts_ref, me, s, owners)
        for r in range(0, cap, 64):
            place = lax.broadcasted_iota(I32, (64, 128), 0) + r
            name = jnp.where(place < count, place + start, -1)
            for c in range(0, examples, 128):
                total = jnp.zeros((64, 128), F32)
                for l in range(looks):
                    total = total + jnp.where(slots_ref[l:l + 1, c:c + 128] == name, 1.0, 0.0)
                named_ref[s * cap + r:s * cap + r + 64, c:c + 128] = total.astype(BF16)


def clip_kernel(owners, *refs):
    messages = refs[:owners]
    pooled_ref, delta_ref, _, clip_ref, scaled_ref, theirs_ref, wide_ref = refs[owners:]
    examples, emb = pooled_ref.shape
    half = theirs_ref.shape[0]
    core = lax.rem(lax.axis_index("dp"), 2)
    norm_sq = messages[0][:, :examples]
    for message in messages[1:]:
        norm_sq = norm_sq + message[:, :examples]
    clip = jnp.minimum(1.0, CLIP_NORM / jnp.sqrt(norm_sq + EPSILON))
    clip_ref[...] = clip
    wide_ref[...] = pooled_ref[...].astype(F32).T * clip
    other = wide_ref[pl.ds((1 - core) * half, half), :].astype(BF16)
    theirs_ref[...] = jnp.dot(other, delta_ref[...], preferred_element_type=F32)
    scaled_ref[...] = wide_ref[pl.ds(core * half, half), :].astype(BF16)


def mine_kernel(scaled_ref, delta_ref, mine_ref):
    mine_ref[...] = jnp.dot(scaled_ref[...], delta_ref[...], preferred_element_type=F32)


def unique_kernel(owners, named_ref, xgrad_ref, clip_ref, gate_ref, *out_refs):
    del gate_ref
    emb = xgrad_ref.shape[0]
    cap = named_ref.shape[0] // owners
    wide = xgrad_ref[...] * clip_ref[...]
    hi = wide.astype(BF16)
    lo = (wide - hi.astype(F32)).astype(BF16)
    terms = jnp.concatenate([hi, lo], axis=0)
    for s in range(owners):
        both = lax.dot_general(
            named_ref[s * cap:(s + 1) * cap, :], terms, (((1,), (1,)), ((), ())),
            preferred_element_type=F32,
        )
        out_refs[s][...] = both[:, :emb] + both[:, emb:]


def place_kernel(owners, *refs):
    pieces, messages = refs[:owners], refs[owners:2 * owners]
    own_ref, table_ref, dense_ref, rows_ref, sems = refs[2 * owners:]
    cap, emb = pieces[0].shape
    half = own_ref.shape[0]
    me, core = lax.axis_index("mp"), lax.rem(lax.axis_index("dp"), 2)
    copy = pltpu.make_async_copy(own_ref, dense_ref.at[pl.ds(core * half, half)], sems.at[owners])
    copy.start()
    copies = [copy]
    row = lax.broadcasted_iota(I32, (ROWS_DEV, cap), 0).astype(F32)
    for s in range(owners):
        ids = messages[s][:, messages[s].shape[1] - cap:]
        hot = jnp.where(row == ids, 1.0, 0.0).astype(BF16)
        wide = pieces[s][...]
        hi = wide.astype(BF16)
        lo = (wide - hi.astype(F32)).astype(BF16)
        both = jnp.dot(hot, jnp.concatenate([hi, lo], axis=1), preferred_element_type=F32)
        rows_ref[s] = both[:, :emb] + both[:, emb:]
        copy = pltpu.make_async_copy(
            rows_ref.at[s], table_ref.at[peer_from(me, s, owners)], sems.at[s]
        )
        copy.start()
        copies.append(copy)
    for copy in copies:
        copy.wait()


def finish_kernel(_, other_ref, dense_ref, sem):
    half = other_ref.shape[0]
    core = lax.rem(lax.axis_index("dp"), 2)
    copy = pltpu.make_async_copy(other_ref, dense_ref.at[pl.ds((1 - core) * half, half)], sem)
    copy.start()
    copy.wait()


def on_device(pooled, delta, w_first, lookup_slot, row_ids, send_counts):
    owners, n_dp = lax.axis_size("mp"), lax.axis_size("dp")
    examples, emb = pooled.shape
    hid = delta.shape[1]
    width = row_ids.shape[-1]
    cap = width // owners
    slots = lookup_slot[:, 0, :].T
    looks = slots.shape[0]
    counts, ids = send_counts[0], row_ids[0]
    half, part = emb // 2, emb // 8

    xgrad, delta, pooled, slots, *messages = call(
        functools.partial(first_kernel, owners),
        [((emb, examples), F32), (delta.shape, BF16), (pooled.shape, BF16), (slots.shape, I32)]
        + [((1, examples + cap), F32)] * owners,
        2 * emb * examples * hid,
        *[pltpu.with_memory_space_constraint(a, pltpu.HBM) for a in (counts, delta, w_first, pooled, slots, ids)],
        specs=[HBM] * 6,
        scratch=[
            pltpu.VMEM(w_first.shape, BF16), pltpu.VMEM(ids.shape, I32),
            pltpu.SMEM(counts.shape, I32), pltpu.SemaphoreType.DMA((5 + examples // CHUNK,)),
        ],
    )
    steps = pairings(owners)
    for s in range(1, owners):
        messages[s] = lax.ppermute(messages[s], "mp", steps[s - 1])
    (named,) = call(
        functools.partial(named_kernel, owners), [((width, examples), BF16)],
        8 * width * examples * looks, counts, slots, specs=[SMEM, VMEM],
    )
    clip, scaled, theirs = call(
        functools.partial(clip_kernel, owners),
        [((1, examples), F32), ((half, examples), BF16), ((half, hid), F32)],
        2 * half * examples * hid,
        *messages, pooled, delta, named,
        specs=[VMEM] * (owners + 2) + [ANY],
        scratch=[pltpu.VMEM((emb, examples), F32)],
    )
    me = lax.axis_index("dp")
    core, chip = me & 1, me >> 1
    swap = [(i, i ^ 1) for i in range(n_dp)]
    came = lax.ppermute(theirs, "dp", swap)
    (mine,) = call(mine_kernel, [((half, hid), F32)], 2 * half * examples * hid, scaled, delta)
    mine = mine + came

    def chips(piece, s):
        return lax.ppermute(piece, "dp", [(i, i ^ (2 * s)) for i in range(n_dp)])

    unique = call(
        functools.partial(unique_kernel, owners), [((cap, emb), F32)] * owners,
        4 * width * examples * emb, named, xgrad, clip, mine, specs=[VMEM] * 3 + [ANY],
    )
    if n_dp == 8:
        got = {}
        for s in (3, 1, 2):
            got[s] = chips(lax.dynamic_slice_in_dim(mine, (chip ^ s) * part, part, 0), s)
        got, _ = lax.optimization_barrier((got, unique[0]))
        total = lax.dynamic_slice_in_dim(mine, chip * part, part, 0) + got[1] + got[2] + got[3]
        own = lax.dynamic_update_slice_in_dim(jnp.zeros((half, hid), F32), total, chip * part, 0)
        for s in (3, 1, 2):
            own = lax.dynamic_update_slice_in_dim(own, chips(total, s), (chip ^ s) * part, 0)
    else:
        own = lax.psum(mine, "dp", axis_index_groups=[list(range(c, n_dp, 2)) for c in (0, 1)])
    for s in range(1, owners):
        unique[s] = lax.ppermute(unique[s], "mp", steps[s - 1])
    own, *unique = lax.optimization_barrier((own, *unique))
    other = lax.ppermute(own, "dp", swap)
    table_grad, dense_grad = call(
        functools.partial(place_kernel, owners),
        [((owners, ROWS_DEV, emb), F32), ((emb, hid), F32)],
        4 * owners * ROWS_DEV * cap * emb, *unique, *messages, own, out_specs=[HBM, HBM],
        scratch=[pltpu.VMEM((owners, ROWS_DEV, emb), F32), pltpu.SemaphoreType.DMA((owners + 1,))],
    )
    (dense_grad,) = call(
        finish_kernel, [((emb, hid), F32)], 0, dense_grad, other, specs=[HBM, VMEM],
        out_specs=[HBM], scratch=[pltpu.SemaphoreType.DMA(())], aliases={0: 0},
    )
    return (dense_grad, table_grad[None])


def solution(mesh):
    placed = (
        P("dp", "mp"),
        P("dp", None),
        P("mp", None),
        P("dp", "mp", None),
        P("dp", "mp", None),
        P("dp", "mp", None),
    )
    return jax.shard_map(
        on_device,
        mesh=mesh,
        in_specs=placed,
        out_specs=(P("mp", None), P("dp", None, "mp", None)),
        check_vma=False,
    )
```

```python
import functools

import jax
import jax.numpy as jnp
from jax import lax
from jax.experimental import pallas as pl
from jax.experimental.pallas import tpu as pltpu
from jax.sharding import PartitionSpec as P

ROWS_DEV = 512
CLIP_NORM = 8.0
EPSILON = 1e-06

VMEM = pl.BlockSpec(memory_space=pltpu.VMEM)
SMEM = pl.BlockSpec(memory_space=pltpu.SMEM)
HBM = pl.BlockSpec(memory_space=pltpu.HBM)
ANY = pl.BlockSpec(memory_space=pl.ANY)
CHUNK = 256
F32, BF16, I32 = jnp.float32, jnp.bfloat16, jnp.int32


def pairings(n):
    if n & (n - 1) == 0:
        return [[(i, i ^ s) for i in range(n)] for s in range(1, n)]
    return [[(i, (i + s) % n) for i in range(n)] for s in range(1, n)]


def peer_to(me, s, n):
    return me ^ s if n & (n - 1) == 0 else lax.rem(me + s, n)


def peer_from(me, s, n):
    return me ^ s if n & (n - 1) == 0 else lax.rem(me + n - s, n)


def call(kernel, outs, flops, *args, specs=None, out_specs=None, scratch=(), aliases=None):
    size = sum(a.size * a.dtype.itemsize for a in args)
    return list(pl.pallas_call(
        kernel,
        out_shape=[jax.ShapeDtypeStruct(shape, dtype) for shape, dtype in outs],
        in_specs=specs or [VMEM] * len(args),
        out_specs=out_specs or [VMEM] * len(outs),
        scratch_shapes=list(scratch),
        input_output_aliases=aliases or {},
        compiler_params=pltpu.CompilerParams(vmem_limit_bytes=16 * 2**20),
        cost_estimate=pl.CostEstimate(flops=flops, bytes_accessed=size, transcendentals=0),
    )(*args))


def window(counts_ref, me, s, owners):
    owner = peer_to(me, s, owners)
    start, count = jnp.int32(0), jnp.int32(0)
    for o in range(owners):
        here = counts_ref[0, o]
        start = start + jnp.where(o < owner, here, 0)
        count = count + jnp.where(o == owner, here, 0)
    return start, count


def first_kernel(owners, counts_hbm, delta_hbm, w_hbm, pooled_hbm, slots_hbm, ids_hbm, *refs):
    xgrad_ref, delta_ref, pooled_ref, slots_ref, *rest = refs
    message_refs, (w_ref, ids_ref, counts_ref, sems) = rest[:owners], rest[owners:]
    examples, emb = pooled_ref.shape
    hid = delta_ref.shape[1]
    looks = slots_ref.shape[0]
    width = ids_ref.shape[1]
    cap = width // owners
    blocks = list(range(0, examples, CHUNK))
    pairs = [(w_hbm, w_ref)]
    pairs += [(delta_hbm.at[pl.ds(r, CHUNK)], delta_ref.at[pl.ds(r, CHUNK)]) for r in blocks]
    pairs += [(counts_hbm, counts_ref), (slots_hbm, slots_ref), (ids_hbm, ids_ref), (pooled_hbm, pooled_ref)]
    copies = [pltpu.make_async_copy(a, b, sems.at[i]) for i, (a, b) in enumerate(pairs)]
    for copy in copies:
        copy.start()
    me = lax.axis_index("mp")
    n = len(blocks)
    copies[0].wait()
    norms = []
    for i, r in enumerate(blocks):
        copies[1 + i].wait()
        xgrad = lax.dot_general(
            w_ref[...], delta_ref[r:r + CHUNK, :], (((1,), (1,)), ((), ())),
            preferred_element_type=F32,
        )
        xgrad_ref[:, r:r + CHUNK] = xgrad
        sums = []
        for q in range(r, r + CHUNK, 128):
            total = jnp.zeros((128, 128), F32)
            for c in range(0, hid, 128):
                piece = delta_ref[q:q + 128, c:c + 128].astype(F32)
                total = total + piece * piece
            sums.append(jnp.sum(total.T, axis=0, keepdims=True))
        norms.append((jnp.sum(xgrad * xgrad, axis=0, keepdims=True), jnp.concatenate(sums, axis=1)))
    for copy in copies[1 + n:]:
        copy.wait()
    slots = slots_ref[...]
    same = jnp.full(slots.shape, 1.0, F32)
    for shift in range(1, looks):
        same = same + jnp.where(slots == pltpu.roll(slots, shift, 0), 1.0, 0.0)
    repeats = jnp.sum(same, axis=0, keepdims=True)
    for i, r in enumerate(blocks):
        xgrad_sq, delta_sq = norms[i]
        sums = []
        for q in range(r, r + CHUNK, 128):
            piece = pooled_ref[q:q + 128, :].astype(F32)
            sums.append(jnp.sum((piece * piece).T, axis=0, keepdims=True))
        partial = delta_sq * jnp.concatenate(sums, axis=1) + repeats[:, r:r + CHUNK] * xgrad_sq
        for message in message_refs:
            message[:, r:r + CHUNK] = partial
    ids = jnp.broadcast_to(ids_ref[...], (8, width))
    place = lax.broadcasted_iota(I32, (1, cap), 1)
    for s in range(owners):
        start, count = window(counts_ref, me, s, owners)
        mine = pltpu.roll(ids, lax.rem(width - start, width), 1)[0:1, :cap]
        message_refs[s][:, examples:] = jnp.where(place < count, mine, -1).astype(F32)


def named_kernel(owners, counts_ref, slots_ref, pooled_ref, named_ref, turned_ref):
    turned_ref[...] = pooled_ref[...].astype(F32).T
    width = named_ref.shape[0]
    looks, examples = slots_ref.shape
    cap = width // owners
    me = lax.axis_index("mp")
    for s in range(owners):
        start, count = window(counts_ref, me, s, owners)
        for r in range(0, cap, 64):
            place = lax.broadcasted_iota(I32, (64, 128), 0) + r
            name = jnp.where(place < count, place + start, -1)
            for c in range(0, examples, 128):
                total = jnp.zeros((64, 128), F32)
                for l in range(looks):
                    total = total + jnp.where(slots_ref[l:l + 1, c:c + 128] == name, 1.0, 0.0)
                named_ref[s * cap + r:s * cap + r + 64, c:c + 128] = total.astype(BF16)


def clip_kernel(owners, *refs):
    messages = refs[:owners]
    turned_ref, delta_ref, _, clip_ref, scaled_ref, theirs_ref, wide_ref = refs[owners:]
    examples = turned_ref.shape[1]
    half = theirs_ref.shape[0]
    core = lax.rem(lax.axis_index("dp"), 2)
    norm_sq = messages[0][:, :examples]
    for message in messages[1:]:
        norm_sq = norm_sq + message[:, :examples]
    clip = jnp.minimum(1.0, CLIP_NORM / jnp.sqrt(norm_sq + EPSILON))
    clip_ref[...] = clip
    wide_ref[...] = turned_ref[...] * clip
    other = wide_ref[pl.ds((1 - core) * half, half), :].astype(BF16)
    theirs_ref[...] = jnp.dot(other, delta_ref[...], preferred_element_type=F32)
    scaled_ref[...] = wide_ref[pl.ds(core * half, half), :].astype(BF16)


def mine_kernel(scaled_ref, delta_ref, mine_ref):
    mine_ref[...] = jnp.dot(scaled_ref[...], delta_ref[...], preferred_element_type=F32)


def split_kernel(steps, mine_ref, came_ref, *part_refs):
    part = part_refs[0].shape[0]
    chip = lax.axis_index("dp") // 2
    for step, out_ref in zip(steps, part_refs):
        rows = pl.ds((chip ^ step) * part, part)
        out_ref[...] = mine_ref[rows, :] + came_ref[rows, :]


def unique_kernel(owners, named_ref, xgrad_ref, clip_ref, gate_ref, *out_refs):
    del gate_ref
    emb = xgrad_ref.shape[0]
    cap = named_ref.shape[0] // owners
    wide = xgrad_ref[...] * clip_ref[...]
    hi = wide.astype(BF16)
    lo = (wide - hi.astype(F32)).astype(BF16)
    terms = jnp.concatenate([hi, lo], axis=0)
    for s in range(owners):
        both = lax.dot_general(
            named_ref[s * cap:(s + 1) * cap, :], terms, (((1,), (1,)), ((), ())),
            preferred_element_type=F32,
        )
        out_refs[s][...] = both[:, :emb] + both[:, emb:]


def place_kernel(owners, *refs):
    pieces, messages = refs[:owners], refs[owners:2 * owners]
    own_ref, table_ref, dense_ref, rows_ref, sems = refs[2 * owners:]
    cap, emb = pieces[0].shape
    half = own_ref.shape[0]
    me, core = lax.axis_index("mp"), lax.rem(lax.axis_index("dp"), 2)
    copy = pltpu.make_async_copy(own_ref, dense_ref.at[pl.ds(core * half, half)], sems.at[owners])
    copy.start()
    copies = [copy]
    row = lax.broadcasted_iota(I32, (ROWS_DEV, cap), 0).astype(F32)
    for s in range(owners):
        ids = messages[s][:, messages[s].shape[1] - cap:]
        hot = jnp.where(row == ids, 1.0, 0.0).astype(BF16)
        wide = pieces[s][...]
        hi = wide.astype(BF16)
        lo = (wide - hi.astype(F32)).astype(BF16)
        both = jnp.dot(hot, jnp.concatenate([hi, lo], axis=1), preferred_element_type=F32)
        rows_ref[s] = both[:, :emb] + both[:, emb:]
        copy = pltpu.make_async_copy(
            rows_ref.at[s], table_ref.at[peer_from(me, s, owners)], sems.at[s]
        )
        copy.start()
        copies.append(copy)
    for copy in copies:
        copy.wait()


def finish_kernel(_, other_ref, dense_ref, sem):
    half = other_ref.shape[0]
    core = lax.rem(lax.axis_index("dp"), 2)
    copy = pltpu.make_async_copy(other_ref, dense_ref.at[pl.ds((1 - core) * half, half)], sem)
    copy.start()
    copy.wait()


def on_device(pooled, delta, w_first, lookup_slot, row_ids, send_counts):
    owners, n_dp = lax.axis_size("mp"), lax.axis_size("dp")
    examples, emb = pooled.shape
    hid = delta.shape[1]
    width = row_ids.shape[-1]
    cap = width // owners
    slots = lookup_slot[:, 0, :].T
    looks = slots.shape[0]
    counts, ids = send_counts[0], row_ids[0]
    half, part = emb // 2, emb // 8

    xgrad, delta, pooled, slots, *messages = call(
        functools.partial(first_kernel, owners),
        [((emb, examples), F32), (delta.shape, BF16), (pooled.shape, BF16), (slots.shape, I32)]
        + [((1, examples + cap), F32)] * owners,
        2 * emb * examples * hid,
        *[pltpu.with_memory_space_constraint(a, pltpu.HBM) for a in (counts, delta, w_first, pooled, slots, ids)],
        specs=[HBM] * 6,
        scratch=[
            pltpu.VMEM(w_first.shape, BF16), pltpu.VMEM(ids.shape, I32),
            pltpu.SMEM(counts.shape, I32), pltpu.SemaphoreType.DMA((5 + examples // CHUNK,)),
        ],
    )
    steps = pairings(owners)
    for s in range(1, owners):
        messages[s] = lax.ppermute(messages[s], "mp", steps[s - 1])
    named, turned = call(
        functools.partial(named_kernel, owners),
        [((width, examples), BF16), ((emb, examples), F32)],
        8 * width * examples * looks, counts, slots, pooled, specs=[SMEM, VMEM, VMEM],
    )
    clip, scaled, theirs = call(
        functools.partial(clip_kernel, owners),
        [((1, examples), F32), ((half, examples), BF16), ((half, hid), F32)],
        2 * half * examples * hid,
        *messages, turned, delta, named,
        specs=[VMEM] * (owners + 2) + [ANY],
        scratch=[pltpu.VMEM((emb, examples), F32)],
    )
    me = lax.axis_index("dp")
    chip = me >> 1
    swap = [(i, i ^ 1) for i in range(n_dp)]
    came = lax.ppermute(theirs, "dp", swap)
    (mine,) = call(mine_kernel, [((half, hid), F32)], 2 * half * examples * hid, scaled, delta)

    def chips(piece, s):
        return lax.ppermute(piece, "dp", [(i, i ^ (2 * s)) for i in range(n_dp)])

    hops = (0, 3, 1, 2)
    if n_dp == 8:
        parts = call(
            functools.partial(split_kernel, hops), [((part, hid), F32)] * 4, half * hid, mine, came
        )
    else:
        parts = [mine + came]
    unique = call(
        functools.partial(unique_kernel, owners), [((cap, emb), F32)] * owners,
        4 * width * examples * emb, named, xgrad, clip, parts[0], specs=[VMEM] * 3 + [ANY],
    )
    for s in range(1, owners):
        unique[s] = lax.ppermute(unique[s], "mp", steps[s - 1])
    if n_dp == 8:
        got = [chips(piece, s) for piece, s in zip(parts[1:], hops[1:])]
        got, unique[0] = lax.optimization_barrier((got, unique[0]))
        total = parts[0] + got[0] + got[1] + got[2]
        own = lax.dynamic_update_slice_in_dim(jnp.zeros((half, hid), F32), total, chip * part, 0)
        own, *unique = lax.optimization_barrier((own, *unique))
        for s in hops[1:]:
            own = lax.dynamic_update_slice_in_dim(own, chips(total, s), (chip ^ s) * part, 0)
    else:
        groups = [list(range(c, n_dp, 2)) for c in (0, 1)]
        own = lax.psum(parts[0], "dp", axis_index_groups=groups)
    other = lax.ppermute(own, "dp", swap)
    table_grad, dense_grad = call(
        functools.partial(place_kernel, owners),
        [((owners, ROWS_DEV, emb), F32), ((emb, hid), F32)],
        4 * owners * ROWS_DEV * cap * emb, *unique, *messages, own, out_specs=[HBM, HBM],
        scratch=[pltpu.VMEM((owners, ROWS_DEV, emb), F32), pltpu.SemaphoreType.DMA((owners + 1,))],
    )
    (dense_grad,) = call(
        finish_kernel, [((emb, hid), F32)], 0, dense_grad, other, specs=[HBM, VMEM],
        out_specs=[HBM], scratch=[pltpu.SemaphoreType.DMA(())], aliases={0: 0},
    )
    return (dense_grad, table_grad[None])


def solution(mesh):
    placed = (
        P("dp", "mp"),
        P("dp", None),
        P("mp", None),
        P("dp", "mp", None),
        P("dp", "mp", None),
        P("dp", "mp", None),
    )
    return jax.shard_map(
        on_device,
        mesh=mesh,
        in_specs=placed,
        out_specs=(P("mp", None), P("dp", None, "mp", None)),
        check_vma=False,
    )
```

```python
import functools

import jax
import jax.numpy as jnp
from jax import lax
from jax.experimental import pallas as pl
from jax.experimental.pallas import tpu as pltpu
from jax.sharding import PartitionSpec as P

ROWS_DEV = 512
CLIP_NORM = 8.0
EPSILON = 1e-06

VMEM = pl.BlockSpec(memory_space=pltpu.VMEM)
SMEM = pl.BlockSpec(memory_space=pltpu.SMEM)
HBM = pl.BlockSpec(memory_space=pltpu.HBM)
ANY = pl.BlockSpec(memory_space=pl.ANY)
CHUNK = 256
F32, BF16, I32 = jnp.float32, jnp.bfloat16, jnp.int32


def pairings(n):
    if n & (n - 1) == 0:
        return [[(i, i ^ s) for i in range(n)] for s in range(1, n)]
    return [[(i, (i + s) % n) for i in range(n)] for s in range(1, n)]


def rounds(n):
    return pairings(n)[::-1]


def peer_to(me, s, n):
    return me ^ s if n & (n - 1) == 0 else lax.rem(me + s, n)


def peer_from(me, s, n):
    return me ^ s if n & (n - 1) == 0 else lax.rem(me + n - s, n)


def call(kernel, outs, flops, *args, specs=None, out_specs=None, scratch=(), aliases=None):
    size = sum(a.size * a.dtype.itemsize for a in args)
    return list(pl.pallas_call(
        kernel,
        out_shape=[jax.ShapeDtypeStruct(shape, dtype) for shape, dtype in outs],
        in_specs=specs or [VMEM] * len(args),
        out_specs=out_specs or [VMEM] * len(outs),
        scratch_shapes=list(scratch),
        input_output_aliases=aliases or {},
        compiler_params=pltpu.CompilerParams(vmem_limit_bytes=16 * 2**20),
        cost_estimate=pl.CostEstimate(flops=flops, bytes_accessed=size, transcendentals=0),
    )(*args))


def window(counts_ref, me, s, owners):
    owner = peer_to(me, s, owners)
    start, count = jnp.int32(0), jnp.int32(0)
    for o in range(owners):
        here = counts_ref[0, o]
        start = start + jnp.where(o < owner, here, 0)
        count = count + jnp.where(o == owner, here, 0)
    return start, count


def first_kernel(delta_hbm, w_hbm, pooled_hbm, slots_hbm, *refs):
    xgrad_ref, delta_ref, pooled_ref, slots_ref, partial_ref, w_ref, sems = refs
    examples, emb = pooled_ref.shape
    hid = delta_ref.shape[1]
    looks = slots_ref.shape[0]
    blocks = list(range(0, examples, CHUNK))
    pairs = [(w_hbm, w_ref)]
    pairs += [(delta_hbm.at[pl.ds(r, CHUNK)], delta_ref.at[pl.ds(r, CHUNK)]) for r in blocks]
    pairs += [(slots_hbm, slots_ref), (pooled_hbm, pooled_ref)]
    copies = [pltpu.make_async_copy(a, b, sems.at[i]) for i, (a, b) in enumerate(pairs)]
    for copy in copies:
        copy.start()
    n = len(blocks)
    copies[0].wait()
    norms = []
    for i, r in enumerate(blocks):
        copies[1 + i].wait()
        xgrad = lax.dot_general(
            w_ref[...], delta_ref[r:r + CHUNK, :], (((1,), (1,)), ((), ())),
            preferred_element_type=F32,
        )
        xgrad_ref[:, r:r + CHUNK] = xgrad
        sums = []
        for q in range(r, r + CHUNK, 128):
            total = jnp.zeros((128, 128), F32)
            for c in range(0, hid, 128):
                piece = delta_ref[q:q + 128, c:c + 128].astype(F32)
                total = total + piece * piece
            sums.append(jnp.sum(total.T, axis=0, keepdims=True))
        norms.append((jnp.sum(xgrad * xgrad, axis=0, keepdims=True), jnp.concatenate(sums, axis=1)))
    for copy in copies[1 + n:]:
        copy.wait()
    slots = slots_ref[...]
    same = jnp.full(slots.shape, 1.0, F32)
    for shift in range(1, looks):
        same = same + jnp.where(slots == pltpu.roll(slots, shift, 0), 1.0, 0.0)
    repeats = jnp.sum(same, axis=0, keepdims=True)
    for i, r in enumerate(blocks):
        xgrad_sq, delta_sq = norms[i]
        sums = []
        for q in range(r, r + CHUNK, 128):
            piece = pooled_ref[q:q + 128, :].astype(F32)
            sums.append(jnp.sum((piece * piece).T, axis=0, keepdims=True))
        partial = delta_sq * jnp.concatenate(sums, axis=1) + repeats[:, r:r + CHUNK] * xgrad_sq
        partial_ref[:, r:r + CHUNK] = partial


def named_kernel(owners, counts_ref, slots_ref, pooled_ref, ids_ref, named_ref, turned_ref, targets_ref):
    turned_ref[...] = pooled_ref[...].astype(F32).T
    width = named_ref.shape[0]
    ids = jnp.broadcast_to(ids_ref[...], (8, width))
    looks, examples = slots_ref.shape
    cap = width // owners
    me = lax.axis_index("mp")
    for s in range(owners):
        start, count = window(counts_ref, me, s, owners)
        mine = pltpu.roll(ids, lax.rem(width - start, width), 1)[0:1, :cap]
        inside = lax.broadcasted_iota(I32, (1, cap), 1) < count
        targets_ref[s] = jnp.where(inside, mine, -1).astype(F32)
        for r in range(0, cap, 64):
            place = lax.broadcasted_iota(I32, (64, 128), 0) + r
            name = jnp.where(place < count, place + start, -1)
            for c in range(0, examples, 128):
                total = jnp.zeros((64, 128), F32)
                for l in range(looks):
                    total = total + jnp.where(slots_ref[l:l + 1, c:c + 128] == name, 1.0, 0.0)
                named_ref[s * cap + r:s * cap + r + 64, c:c + 128] = total.astype(BF16)


def clip_kernel(*refs):
    *messages, turned_ref, delta_ref, _, clip_ref, scaled_ref, theirs_ref, wide_ref = refs
    half = theirs_ref.shape[0]
    core = lax.rem(lax.axis_index("dp"), 2)
    norm_sq = messages[0][...]
    for message in messages[1:]:
        norm_sq = norm_sq + message[...]
    clip = jnp.minimum(1.0, CLIP_NORM / jnp.sqrt(norm_sq + EPSILON))
    clip_ref[...] = clip
    wide_ref[...] = turned_ref[...] * clip
    other = wide_ref[pl.ds((1 - core) * half, half), :].astype(BF16)
    theirs_ref[...] = jnp.dot(other, delta_ref[...], preferred_element_type=F32)
    scaled_ref[...] = wide_ref[pl.ds(core * half, half), :].astype(BF16)


def mine_kernel(scaled_ref, delta_ref, mine_ref):
    mine_ref[...] = jnp.dot(scaled_ref[...], delta_ref[...], preferred_element_type=F32)


def split_kernel(steps, mine_ref, came_ref, *part_refs):
    part = part_refs[0].shape[0]
    chip = lax.axis_index("dp") // 2
    for step, out_ref in zip(steps, part_refs):
        rows = pl.ds((chip ^ step) * part, part)
        out_ref[...] = mine_ref[rows, :] + came_ref[rows, :]


def unique_kernel(owners, named_ref, xgrad_ref, clip_ref, targets_ref, _, *out_refs):
    emb = xgrad_ref.shape[0]
    cap = named_ref.shape[0] // owners
    wide = xgrad_ref[...] * clip_ref[...]
    hi = wide.astype(BF16)
    lo = (wide - hi.astype(F32)).astype(BF16)
    terms = jnp.concatenate([hi, lo], axis=0)
    for s in range(owners):
        both = lax.dot_general(
            named_ref[s * cap:(s + 1) * cap, :], terms, (((1,), (1,)), ((), ())),
            preferred_element_type=F32,
        )
        out_refs[s][:cap, :] = both[:, :emb] + both[:, emb:]
        out_refs[s][cap:, :] = jnp.zeros((out_refs[s].shape[0] - cap, emb), F32)
        for q in range(cap // emb):
            out_refs[s][cap + q:cap + q + 1, :] = targets_ref[s, :, q * emb:(q + 1) * emb]


def place_kernel(owners, cap, *refs):
    pieces = refs[:owners]
    own_ref, table_ref, dense_ref, rows_ref, sems = refs[owners:]
    emb = pieces[0].shape[1]
    half = own_ref.shape[0]
    me, core = lax.axis_index("mp"), lax.rem(lax.axis_index("dp"), 2)
    copy = pltpu.make_async_copy(own_ref, dense_ref.at[pl.ds(core * half, half)], sems.at[owners])
    copy.start()
    copies = [copy]
    row = lax.broadcasted_iota(I32, (ROWS_DEV, cap), 0).astype(F32)
    for s in range(owners):
        ids = [pieces[s][cap + q:cap + q + 1, :] for q in range(cap // emb)]
        ids = jnp.concatenate(ids, axis=1)
        hot = jnp.where(row == ids, 1.0, 0.0).astype(BF16)
        wide = pieces[s][:cap, :]
        hi = wide.astype(BF16)
        lo = (wide - hi.astype(F32)).astype(BF16)
        both = jnp.dot(hot, jnp.concatenate([hi, lo], axis=1), preferred_element_type=F32)
        rows_ref[s] = both[:, :emb] + both[:, emb:]
        copy = pltpu.make_async_copy(
            rows_ref.at[s], table_ref.at[peer_from(me, s, owners)], sems.at[s]
        )
        copy.start()
        copies.append(copy)
    for copy in copies:
        copy.wait()


def finish_kernel(_, other_ref, dense_ref, sem):
    half = other_ref.shape[0]
    core = lax.rem(lax.axis_index("dp"), 2)
    copy = pltpu.make_async_copy(other_ref, dense_ref.at[pl.ds((1 - core) * half, half)], sem)
    copy.start()
    copy.wait()


def on_device(pooled, delta, w_first, lookup_slot, row_ids, send_counts):
    owners, n_dp = lax.axis_size("mp"), lax.axis_size("dp")
    examples, emb = pooled.shape
    hid = delta.shape[1]
    width = row_ids.shape[-1]
    cap = width // owners
    slots = lookup_slot[:, 0, :].T
    looks = slots.shape[0]
    counts, ids = send_counts[0], row_ids[0]
    half, part = emb // 2, emb // 8
    tail = -(-cap // (8 * emb)) * 8

    xgrad, delta, pooled, slots, partial = call(
        first_kernel,
        [((emb, examples), F32), (delta.shape, BF16), (pooled.shape, BF16), (slots.shape, I32)]
        + [((1, examples), F32)],
        2 * emb * examples * hid,
        *[pltpu.with_memory_space_constraint(a, pltpu.HBM) for a in (delta, w_first, pooled, slots)],
        specs=[HBM] * 4,
        scratch=[pltpu.VMEM(w_first.shape, BF16), pltpu.SemaphoreType.DMA((3 + examples // CHUNK,))],
    )
    norms = [lax.ppermute(partial, "mp", r) for r in rounds(owners)]
    named, turned, targets = call(
        functools.partial(named_kernel, owners),
        [((width, examples), BF16), ((emb, examples), F32), ((owners, 1, cap), F32)],
        8 * width * examples * looks, counts, slots, pooled, ids, specs=[SMEM, VMEM, VMEM, VMEM],
    )
    clip, scaled, theirs = call(
        clip_kernel,
        [((1, examples), F32), ((half, examples), BF16), ((half, hid), F32)],
        2 * half * examples * hid,
        *norms, partial, turned, delta, named,
        specs=[VMEM] * (len(norms) + 3) + [ANY],
        scratch=[pltpu.VMEM((emb, examples), F32)],
    )
    steps = pairings(owners)
    me = lax.axis_index("dp")
    chip = me >> 1
    swap = [(i, i ^ 1) for i in range(n_dp)]
    came = lax.ppermute(theirs, "dp", swap)
    (mine,) = call(mine_kernel, [((half, hid), F32)], 2 * half * examples * hid, scaled, delta)

    def chips(piece, s):
        return lax.ppermute(piece, "dp", [(i, i ^ (2 * s)) for i in range(n_dp)])

    hops = (0, 3, 1, 2)
    if n_dp == 8:
        parts = call(
            functools.partial(split_kernel, hops), [((part, hid), F32)] * 4, half * hid, mine, came
        )
    else:
        parts = [mine + came]
    unique = call(
        functools.partial(unique_kernel, owners), [((cap + tail, emb), F32)] * owners,
        4 * width * examples * emb, named, xgrad, clip, targets, parts[0], specs=[VMEM] * 4 + [ANY],
    )
    for s in range(1, owners):
        unique[s] = lax.ppermute(unique[s], "mp", steps[s - 1])
    if n_dp == 8:
        got = [chips(piece, s) for piece, s in zip(parts[1:], hops[1:])]
        got, unique[0] = lax.optimization_barrier((got, unique[0]))
        total = parts[0] + got[0] + got[1] + got[2]
        own = lax.dynamic_update_slice_in_dim(jnp.zeros((half, hid), F32), total, chip * part, 0)
        own, *unique = lax.optimization_barrier((own, *unique))
        for s in hops[1:]:
            own = lax.dynamic_update_slice_in_dim(own, chips(total, s), (chip ^ s) * part, 0)
    else:
        groups = [list(range(c, n_dp, 2)) for c in (0, 1)]
        own = lax.psum(parts[0], "dp", axis_index_groups=groups)
    other = lax.ppermute(own, "dp", swap)
    table_grad, dense_grad = call(
        functools.partial(place_kernel, owners, cap),
        [((owners, ROWS_DEV, emb), F32), ((emb, hid), F32)],
        4 * owners * ROWS_DEV * cap * emb, *unique, own, out_specs=[HBM, HBM],
        scratch=[pltpu.VMEM((owners, ROWS_DEV, emb), F32), pltpu.SemaphoreType.DMA((owners + 1,))],
    )
    (dense_grad,) = call(
        finish_kernel, [((emb, hid), F32)], 0, dense_grad, other, specs=[HBM, VMEM],
        out_specs=[HBM], scratch=[pltpu.SemaphoreType.DMA(())], aliases={0: 0},
    )
    return (dense_grad, table_grad[None])


def solution(mesh):
    placed = (
        P("dp", "mp"),
        P("dp", None),
        P("mp", None),
        P("dp", "mp", None),
        P("dp", "mp", None),
        P("dp", "mp", None),
    )
    return jax.shard_map(
        on_device,
        mesh=mesh,
        in_specs=placed,
        out_specs=(P("mp", None), P("dp", None, "mp", None)),
        check_vma=False,
    )
```

```python
import functools

import jax
import jax.numpy as jnp
from jax import lax
from jax.experimental import pallas as pl
from jax.experimental.pallas import tpu as pltpu
from jax.sharding import PartitionSpec as P

ROWS_DEV = 512
CLIP_NORM = 8.0
EPSILON = 1e-06

VMEM = pl.BlockSpec(memory_space=pltpu.VMEM)
SMEM = pl.BlockSpec(memory_space=pltpu.SMEM)
HBM = pl.BlockSpec(memory_space=pltpu.HBM)
ANY = pl.BlockSpec(memory_space=pl.ANY)
CHUNK = 256
F32, BF16, I32 = jnp.float32, jnp.bfloat16, jnp.int32


def pairings(n):
    if n & (n - 1) == 0:
        return [[(i, i ^ s) for i in range(n)] for s in range(1, n)]
    return [[(i, (i + s) % n) for i in range(n)] for s in range(1, n)]


def rounds(n):
    return pairings(n)[::-1]


def peer_to(me, s, n):
    return me ^ s if n & (n - 1) == 0 else lax.rem(me + s, n)


def peer_from(me, s, n):
    return me ^ s if n & (n - 1) == 0 else lax.rem(me + n - s, n)


def call(kernel, outs, flops, *args, specs=None, out_specs=None, scratch=(), aliases=None):
    size = sum(a.size * a.dtype.itemsize for a in args)
    return list(pl.pallas_call(
        kernel,
        out_shape=[jax.ShapeDtypeStruct(shape, dtype) for shape, dtype in outs],
        in_specs=specs or [VMEM] * len(args),
        out_specs=out_specs or [VMEM] * len(outs),
        scratch_shapes=list(scratch),
        input_output_aliases=aliases or {},
        compiler_params=pltpu.CompilerParams(vmem_limit_bytes=16 * 2**20),
        cost_estimate=pl.CostEstimate(flops=flops, bytes_accessed=size, transcendentals=0),
    )(*args))


def window(counts_ref, me, s, owners):
    owner = peer_to(me, s, owners)
    start, count = jnp.int32(0), jnp.int32(0)
    for o in range(owners):
        here = counts_ref[0, o]
        start = start + jnp.where(o < owner, here, 0)
        count = count + jnp.where(o == owner, here, 0)
    return start, count


def first_kernel(delta_hbm, w_hbm, pooled_hbm, slots_hbm, *refs):
    xgrad_ref, delta_ref, pooled_ref, slots_ref, partial_ref, w_ref, sems = refs
    examples, emb = pooled_ref.shape
    hid = delta_ref.shape[1]
    looks = slots_ref.shape[0]
    blocks = list(range(0, examples, CHUNK))
    pairs = [(w_hbm, w_ref)]
    pairs += [(delta_hbm.at[pl.ds(r, CHUNK)], delta_ref.at[pl.ds(r, CHUNK)]) for r in blocks]
    pairs += [(slots_hbm, slots_ref), (pooled_hbm, pooled_ref)]
    copies = [pltpu.make_async_copy(a, b, sems.at[i]) for i, (a, b) in enumerate(pairs)]
    for copy in copies:
        copy.start()
    n = len(blocks)
    copies[0].wait()
    norms = []
    for i, r in enumerate(blocks):
        copies[1 + i].wait()
        xgrad = lax.dot_general(
            w_ref[...], delta_ref[r:r + CHUNK, :], (((1,), (1,)), ((), ())),
            preferred_element_type=F32,
        )
        xgrad_ref[:, r:r + CHUNK] = xgrad
        sums = []
        for q in range(r, r + CHUNK, 128):
            total = jnp.zeros((128, 128), F32)
            for c in range(0, hid, 128):
                piece = delta_ref[q:q + 128, c:c + 128].astype(F32)
                total = total + piece * piece
            sums.append(jnp.sum(total.T, axis=0, keepdims=True))
        norms.append((jnp.sum(xgrad * xgrad, axis=0, keepdims=True), jnp.concatenate(sums, axis=1)))
    for copy in copies[1 + n:]:
        copy.wait()
    slots = slots_ref[...]
    same = jnp.full(slots.shape, 1.0, F32)
    for shift in range(1, looks):
        same = same + jnp.where(slots == pltpu.roll(slots, shift, 0), 1.0, 0.0)
    repeats = jnp.sum(same, axis=0, keepdims=True)
    for i, r in enumerate(blocks):
        xgrad_sq, delta_sq = norms[i]
        sums = []
        for q in range(r, r + CHUNK, 128):
            piece = pooled_ref[q:q + 128, :].astype(F32)
            sums.append(jnp.sum((piece * piece).T, axis=0, keepdims=True))
        partial = delta_sq * jnp.concatenate(sums, axis=1) + repeats[:, r:r + CHUNK] * xgrad_sq
        partial_ref[:, r:r + CHUNK] = partial


def named_kernel(owners, counts_ref, slots_ref, pooled_ref, ids_ref, named_ref, turned_ref, targets_ref):
    turned_ref[...] = pooled_ref[...].astype(F32).T
    width = named_ref.shape[0]
    ids = jnp.broadcast_to(ids_ref[...], (8, width))
    looks, examples = slots_ref.shape
    cap = width // owners
    me = lax.axis_index("mp")
    one, zero = jnp.ones((16, 128), BF16), jnp.zeros((16, 128), BF16)
    wide = {}
    for l in range(looks):
        for c in range(0, examples, 128):
            line = jnp.broadcast_to(slots_ref[l:l + 1, c:c + 128], (16, 128))
            wide[l, c // 128] = line.astype(jnp.int16)
    for s in range(owners):
        start, count = window(counts_ref, me, s, owners)
        mine = pltpu.roll(ids, lax.rem(width - start, width), 1)[0:1, :cap]
        inside = lax.broadcasted_iota(I32, (1, cap), 1) < count
        targets_ref[s] = jnp.where(inside, mine, -1).astype(F32)
        for r in range(0, cap, 16):
            place = lax.broadcasted_iota(I32, (16, 128), 0) + r
            name = jnp.where(place < count, place + start, -1).astype(jnp.int16)
            for c in range(0, examples, 128):
                total = jnp.zeros((16, 128), BF16)
                for l in range(looks):
                    total = total + jnp.where(wide[l, c // 128] == name, one, zero)
                named_ref[s * cap + r:s * cap + r + 16, c:c + 128] = total


def clip_kernel(*refs):
    *messages, turned_ref, delta_ref, _, clip_ref, scaled_ref, theirs_ref, wide_ref = refs
    half = theirs_ref.shape[0]
    core = lax.rem(lax.axis_index("dp"), 2)
    norm_sq = messages[0][...]
    for message in messages[1:]:
        norm_sq = norm_sq + message[...]
    clip = jnp.minimum(1.0, CLIP_NORM / jnp.sqrt(norm_sq + EPSILON))
    clip_ref[...] = clip
    wide_ref[...] = turned_ref[...] * clip
    other = wide_ref[pl.ds((1 - core) * half, half), :].astype(BF16)
    theirs_ref[...] = jnp.dot(other, delta_ref[...], preferred_element_type=F32)
    scaled_ref[...] = wide_ref[pl.ds(core * half, half), :].astype(BF16)


def mine_kernel(scaled_ref, delta_ref, mine_ref):
    mine_ref[...] = jnp.dot(scaled_ref[...], delta_ref[...], preferred_element_type=F32)


def split_kernel(steps, mine_ref, came_ref, *part_refs):
    part = part_refs[0].shape[0]
    chip = lax.axis_index("dp") // 2
    for step, out_ref in zip(steps, part_refs):
        rows = pl.ds((chip ^ step) * part, part)
        out_ref[...] = mine_ref[rows, :] + came_ref[rows, :]


def unique_kernel(owners, named_ref, xgrad_ref, clip_ref, targets_ref, _, *out_refs):
    emb = xgrad_ref.shape[0]
    cap = named_ref.shape[0] // owners
    wide = xgrad_ref[...] * clip_ref[...]
    hi = wide.astype(BF16)
    lo = (wide - hi.astype(F32)).astype(BF16)
    terms = jnp.concatenate([hi, lo], axis=0)
    for s in range(owners):
        both = lax.dot_general(
            named_ref[s * cap:(s + 1) * cap, :], terms, (((1,), (1,)), ((), ())),
            preferred_element_type=F32,
        )
        out_refs[s][:cap, :] = both[:, :emb] + both[:, emb:]
        out_refs[s][cap:, :] = jnp.zeros((out_refs[s].shape[0] - cap, emb), F32)
        for q in range(cap // emb):
            out_refs[s][cap + q:cap + q + 1, :] = targets_ref[s, :, q * emb:(q + 1) * emb]


def place_kernel(owners, cap, *refs):
    pieces = refs[:owners]
    own_ref, table_ref, dense_ref, rows_ref, sems = refs[owners:]
    emb = pieces[0].shape[1]
    half = own_ref.shape[0]
    me, core = lax.axis_index("mp"), lax.rem(lax.axis_index("dp"), 2)
    copy = pltpu.make_async_copy(own_ref, dense_ref.at[pl.ds(core * half, half)], sems.at[owners])
    copy.start()
    copies = [copy]
    row = lax.broadcasted_iota(I32, (ROWS_DEV, cap), 0).astype(F32)
    for s in range(owners):
        ids = [pieces[s][cap + q:cap + q + 1, :] for q in range(cap // emb)]
        ids = jnp.concatenate(ids, axis=1)
        hot = jnp.where(row == ids, 1.0, 0.0).astype(BF16)
        wide = pieces[s][:cap, :]
        hi = wide.astype(BF16)
        lo = (wide - hi.astype(F32)).astype(BF16)
        both = jnp.dot(hot, jnp.concatenate([hi, lo], axis=1), preferred_element_type=F32)
        rows_ref[s] = both[:, :emb] + both[:, emb:]
        copy = pltpu.make_async_copy(
            rows_ref.at[s], table_ref.at[peer_from(me, s, owners)], sems.at[s]
        )
        copy.start()
        copies.append(copy)
    for copy in copies:
        copy.wait()


def finish_kernel(_, other_ref, dense_ref, sem):
    half = other_ref.shape[0]
    core = lax.rem(lax.axis_index("dp"), 2)
    copy = pltpu.make_async_copy(other_ref, dense_ref.at[pl.ds((1 - core) * half, half)], sem)
    copy.start()
    copy.wait()


def on_device(pooled, delta, w_first, lookup_slot, row_ids, send_counts):
    owners, n_dp = lax.axis_size("mp"), lax.axis_size("dp")
    examples, emb = pooled.shape
    hid = delta.shape[1]
    width = row_ids.shape[-1]
    cap = width // owners
    slots = lookup_slot[:, 0, :].T
    looks = slots.shape[0]
    counts, ids = send_counts[0], row_ids[0]
    half, part = emb // 2, emb // 8
    tail = -(-cap // (8 * emb)) * 8

    xgrad, delta, pooled, slots, partial = call(
        first_kernel,
        [((emb, examples), F32), (delta.shape, BF16), (pooled.shape, BF16), (slots.shape, I32)]
        + [((1, examples), F32)],
        2 * emb * examples * hid,
        *[pltpu.with_memory_space_constraint(a, pltpu.HBM) for a in (delta, w_first, pooled, slots)],
        specs=[HBM] * 4,
        scratch=[pltpu.VMEM(w_first.shape, BF16), pltpu.SemaphoreType.DMA((3 + examples // CHUNK,))],
    )
    norms = [lax.ppermute(partial, "mp", r) for r in rounds(owners)]
    named, turned, targets = call(
        functools.partial(named_kernel, owners),
        [((width, examples), BF16), ((emb, examples), F32), ((owners, 1, cap), F32)],
        8 * width * examples * looks, counts, slots, pooled, ids, specs=[SMEM, VMEM, VMEM, VMEM],
    )
    clip, scaled, theirs = call(
        clip_kernel,
        [((1, examples), F32), ((half, examples), BF16), ((half, hid), F32)],
        2 * half * examples * hid,
        *norms, partial, turned, delta, named,
        specs=[VMEM] * (len(norms) + 3) + [ANY],
        scratch=[pltpu.VMEM((emb, examples), F32)],
    )
    steps = pairings(owners)
    me = lax.axis_index("dp")
    chip = me >> 1
    swap = [(i, i ^ 1) for i in range(n_dp)]
    came = lax.ppermute(theirs, "dp", swap)
    (mine,) = call(mine_kernel, [((half, hid), F32)], 2 * half * examples * hid, scaled, delta)

    def chips(piece, s):
        return lax.ppermute(piece, "dp", [(i, i ^ (2 * s)) for i in range(n_dp)])

    hops = (0, 2, 3, 1)
    if n_dp == 8:
        parts = call(
            functools.partial(split_kernel, hops), [((part, hid), F32)] * 4, half * hid, mine, came
        )
    else:
        parts = [mine + came]
    unique = call(
        functools.partial(unique_kernel, owners), [((cap + tail, emb), F32)] * owners,
        4 * width * examples * emb, named, xgrad, clip, targets, parts[0], specs=[VMEM] * 4 + [ANY],
    )
    for s in range(1, owners):
        unique[s] = lax.ppermute(unique[s], "mp", steps[s - 1])
    if n_dp == 8:
        got = [chips(piece, s) for piece, s in zip(parts[1:], hops[1:])]
        got, unique[0] = lax.optimization_barrier((got, unique[0]))
        total = parts[0] + got[0] + got[1] + got[2]
        own = lax.dynamic_update_slice_in_dim(jnp.zeros((half, hid), F32), total, chip * part, 0)
        own, *unique = lax.optimization_barrier((own, *unique))
        for s in hops[1:]:
            own = lax.dynamic_update_slice_in_dim(own, chips(total, s), (chip ^ s) * part, 0)
    else:
        groups = [list(range(c, n_dp, 2)) for c in (0, 1)]
        own = lax.psum(parts[0], "dp", axis_index_groups=groups)
    other = lax.ppermute(own, "dp", swap)
    table_grad, dense_grad = call(
        functools.partial(place_kernel, owners, cap),
        [((owners, ROWS_DEV, emb), F32), ((emb, hid), F32)],
        4 * owners * ROWS_DEV * cap * emb, *unique, own, out_specs=[HBM, HBM],
        scratch=[pltpu.VMEM((owners, ROWS_DEV, emb), F32), pltpu.SemaphoreType.DMA((owners + 1,))],
    )
    (dense_grad,) = call(
        finish_kernel, [((emb, hid), F32)], 0, dense_grad, other, specs=[HBM, VMEM],
        out_specs=[HBM], scratch=[pltpu.SemaphoreType.DMA(())], aliases={0: 0},
    )
    return (dense_grad, table_grad[None])


def solution(mesh):
    placed = (
        P("dp", "mp"),
        P("dp", None),
        P("mp", None),
        P("dp", "mp", None),
        P("dp", "mp", None),
        P("dp", "mp", None),
    )
    return jax.shard_map(
        on_device,
        mesh=mesh,
        in_specs=placed,
        out_specs=(P("mp", None), P("dp", None, "mp", None)),
        check_vma=False,
    )
```

```python
import functools

import jax
import jax.numpy as jnp
from jax import lax
from jax.experimental import pallas as pl
from jax.experimental.pallas import tpu as pltpu
from jax.sharding import PartitionSpec as P

ROWS_DEV = 512
CLIP_NORM = 8.0
EPSILON = 1e-06

VMEM = pl.BlockSpec(memory_space=pltpu.VMEM)
SMEM = pl.BlockSpec(memory_space=pltpu.SMEM)
HBM = pl.BlockSpec(memory_space=pltpu.HBM)
ANY = pl.BlockSpec(memory_space=pl.ANY)
CHUNK = 512
F32, BF16, I32 = jnp.float32, jnp.bfloat16, jnp.int32


def pairings(n):
    if n & (n - 1) == 0:
        return [[(i, i ^ s) for i in range(n)] for s in range(1, n)]
    return [[(i, (i + s) % n) for i in range(n)] for s in range(1, n)]


def rounds(n):
    return pairings(n)


def peer_to(me, s, n):
    return me ^ s if n & (n - 1) == 0 else lax.rem(me + s, n)


def peer_from(me, s, n):
    return me ^ s if n & (n - 1) == 0 else lax.rem(me + n - s, n)


def call(kernel, outs, flops, *args, specs=None, out_specs=None, scratch=(), aliases=None):
    size = sum(a.size * a.dtype.itemsize for a in args)
    return list(pl.pallas_call(
        kernel,
        out_shape=[jax.ShapeDtypeStruct(shape, dtype) for shape, dtype in outs],
        in_specs=specs or [VMEM] * len(args),
        out_specs=out_specs or [VMEM] * len(outs),
        scratch_shapes=list(scratch),
        input_output_aliases=aliases or {},
        compiler_params=pltpu.CompilerParams(vmem_limit_bytes=16 * 2**20),
        cost_estimate=pl.CostEstimate(flops=flops, bytes_accessed=size, transcendentals=0),
    )(*args))


def window(counts_ref, me, s, owners):
    owner = peer_to(me, s, owners)
    start, count = jnp.int32(0), jnp.int32(0)
    for o in range(owners):
        here = counts_ref[0, o]
        start = start + jnp.where(o < owner, here, 0)
        count = count + jnp.where(o == owner, here, 0)
    return start, count


def first_kernel(delta_hbm, w_hbm, pooled_hbm, slots_hbm, *refs):
    xgrad_ref, delta_ref, pooled_ref, slots_ref, partial_ref, w_ref, sems = refs
    examples, emb = pooled_ref.shape
    looks = slots_ref.shape[0]
    blocks = list(range(0, examples, CHUNK))
    pairs = [(w_hbm, w_ref)]
    pairs += [(delta_hbm.at[pl.ds(r, CHUNK)], delta_ref.at[pl.ds(r, CHUNK)]) for r in blocks]
    pairs += [(slots_hbm, slots_ref), (pooled_hbm, pooled_ref)]
    copies = [pltpu.make_async_copy(a, b, sems.at[i]) for i, (a, b) in enumerate(pairs)]
    for copy in copies[-2:] + copies[:-2]:
        copy.start()
    n = len(blocks)
    for copy in copies[1 + n:]:
        copy.wait()
    slots = slots_ref[...]
    same = jnp.full(slots.shape, 1.0, F32)
    for shift in range(1, looks):
        same = same + jnp.where(slots == pltpu.roll(slots, shift, 0), 1.0, 0.0)
    repeats = jnp.sum(same, axis=0, keepdims=True)
    copies[0].wait()
    norms = []
    for i, r in enumerate(blocks):
        copies[1 + i].wait()
        xgrad = lax.dot_general(
            w_ref[...], delta_ref[r:r + CHUNK, :], (((1,), (1,)), ((), ())),
            preferred_element_type=F32,
        )
        xgrad_ref[:, r:r + CHUNK] = xgrad
        norms.append(jnp.sum(xgrad * xgrad, axis=0, keepdims=True))
    for i, r in enumerate(blocks):
        sums = []
        for q in range(r, r + CHUNK, 128):
            piece = pooled_ref[q:q + 128, :].astype(F32)
            sums.append(jnp.sum((piece * piece).T, axis=0, keepdims=True))
        partial_ref[0:1, r:r + CHUNK] = jnp.concatenate(sums, axis=1)
        partial_ref[1:2, r:r + CHUNK] = repeats[:, r:r + CHUNK] * norms[i]


def named_kernel(owners, counts_ref, slots_ref, pooled_ref, ids_ref, delta_ref, named_ref, turned_ref, targets_ref, delta_sq_ref):
    for r in range(0, delta_ref.shape[0], 128):
        total = jnp.zeros((128, 128), F32)
        for c in range(0, delta_ref.shape[1], 128):
            piece = delta_ref[r:r + 128, c:c + 128].astype(F32)
            total = total + piece * piece
        delta_sq_ref[:, r:r + 128] = jnp.sum(total.T, axis=0, keepdims=True)
    turned_ref[...] = pooled_ref[...].astype(F32).T
    width = named_ref.shape[0]
    ids = jnp.broadcast_to(ids_ref[...], (8, width))
    looks, examples = slots_ref.shape
    cap = width // owners
    me = lax.axis_index("mp")
    one, zero = jnp.ones((16, 128), BF16), jnp.zeros((16, 128), BF16)
    wide = {}
    for l in range(looks):
        for c in range(0, examples, 128):
            line = jnp.broadcast_to(slots_ref[l:l + 1, c:c + 128], (16, 128))
            wide[l, c // 128] = line.astype(jnp.int16)
    for s in range(owners):
        start, count = window(counts_ref, me, s, owners)
        mine = pltpu.roll(ids, lax.rem(width - start, width), 1)[0:1, :cap]
        inside = lax.broadcasted_iota(I32, (1, cap), 1) < count
        targets_ref[s] = jnp.where(inside, mine, -1).astype(F32)
        for r in range(0, cap, 16):
            place = lax.broadcasted_iota(I32, (16, 128), 0) + r
            name = jnp.where(place < count, place + start, -1).astype(jnp.int16)
            for c in range(0, examples, 128):
                total = jnp.zeros((16, 128), BF16)
                for l in range(looks):
                    total = total + jnp.where(wide[l, c // 128] == name, one, zero)
                named_ref[s * cap + r:s * cap + r + 16, c:c + 128] = total


def clip_kernel(*refs):
    *messages, turned_ref, delta_sq_ref, delta_ref, _, clip_ref, scaled_ref, theirs_ref, wide_ref = refs
    half = theirs_ref.shape[0]
    core = lax.rem(lax.axis_index("dp"), 2)
    total = messages[0][...]
    for message in messages[1:]:
        total = total + message[...]
    norm_sq = delta_sq_ref[...] * total[0:1, :] + total[1:2, :]
    clip = jnp.minimum(1.0, CLIP_NORM / jnp.sqrt(norm_sq + EPSILON))
    clip_ref[...] = clip
    wide_ref[...] = turned_ref[...] * clip
    other = wide_ref[pl.ds((1 - core) * half, half), :].astype(BF16)
    theirs_ref[...] = jnp.dot(other, delta_ref[...], preferred_element_type=F32)
    scaled_ref[...] = wide_ref[pl.ds(core * half, half), :].astype(BF16)


def mine_kernel(scaled_ref, delta_ref, mine_ref):
    mine_ref[...] = jnp.dot(scaled_ref[...], delta_ref[...], preferred_element_type=F32)


def split_kernel(steps, mine_ref, came_ref, *part_refs):
    part = part_refs[0].shape[0]
    chip = lax.axis_index("dp") // 2
    for step, out_ref in zip(steps, part_refs):
        rows = pl.ds((chip ^ step) * part, part)
        out_ref[...] = mine_ref[rows, :] + came_ref[rows, :]


def unique_kernel(owners, named_ref, xgrad_ref, clip_ref, targets_ref, _, *out_refs):
    emb = xgrad_ref.shape[0]
    cap = named_ref.shape[0] // owners
    wide = xgrad_ref[...] * clip_ref[...]
    hi = wide.astype(BF16)
    lo = (wide - hi.astype(F32)).astype(BF16)
    terms = jnp.concatenate([hi, lo], axis=0)
    for s in range(owners):
        both = lax.dot_general(
            named_ref[s * cap:(s + 1) * cap, :], terms, (((1,), (1,)), ((), ())),
            preferred_element_type=F32,
        )
        out_refs[s][:cap, :] = both[:, :emb] + both[:, emb:]
        out_refs[s][cap:, :] = jnp.zeros((out_refs[s].shape[0] - cap, emb), F32)
        for q in range(cap // emb):
            out_refs[s][cap + q:cap + q + 1, :] = targets_ref[s, :, q * emb:(q + 1) * emb]


def place_of(hop, flip, rows, part):
    me = lax.axis_index("dp")
    chip, core = me // 2, lax.rem(me, 2)
    core = 1 - core if flip else core
    return pl.ds(core * (rows // 2) + ((chip ^ hop) * part if 2 * part < rows else 0), part)


def place_kernel(owners, cap, order, *refs):
    pieces = refs[:owners]
    own, ends = refs[owners:owners + len(order)], refs[owners + len(order):-4]
    table_ref, dense_ref, rows_ref, sems = refs[-4:]
    emb = pieces[0].shape[1]
    part = own[0].shape[0]
    me = lax.axis_index("mp")
    places = [(own[i], hop, 0) for i, hop in enumerate(order)]
    for end in ends:
        places += [(end.at[pl.ds(i * part, part)], hop, 1) for i, hop in enumerate(order[:len(order) // 2])]
    copies = []
    for i, (piece, hop, flip) in enumerate(places):
        rows = place_of(hop, flip, dense_ref.shape[0], part)
        copies.append(pltpu.make_async_copy(piece, dense_ref.at[rows], sems.at[owners + i]))
        copies[-1].start()
    row = lax.broadcasted_iota(I32, (ROWS_DEV, cap), 0).astype(F32)
    for s in range(owners):
        ids = [pieces[s][cap + q:cap + q + 1, :] for q in range(cap // emb)]
        ids = jnp.concatenate(ids, axis=1)
        hot = jnp.where(row == ids, 1.0, 0.0).astype(BF16)
        wide = pieces[s][:cap, :]
        hi = wide.astype(BF16)
        lo = (wide - hi.astype(F32)).astype(BF16)
        both = jnp.dot(hot, jnp.concatenate([hi, lo], axis=1), preferred_element_type=F32)
        rows_ref[s] = both[:, :emb] + both[:, emb:]
        copy = pltpu.make_async_copy(
            rows_ref.at[s], table_ref.at[peer_from(me, s, owners)], sems.at[s]
        )
        copy.start()
        copies.append(copy)
    for copy in copies:
        copy.wait()


def finish_kernel(order, _, end_ref, dense_ref, sems):
    part = end_ref.shape[0] // len(order)
    copies = []
    for i, hop in enumerate(order):
        rows = place_of(hop, 1, dense_ref.shape[0], part)
        copies.append(pltpu.make_async_copy(end_ref.at[pl.ds(i * part, part)], dense_ref.at[rows], sems.at[i]))
        copies[-1].start()
    for copy in copies:
        copy.wait()


def on_device(pooled, delta, w_first, lookup_slot, row_ids, send_counts):
    owners, n_dp = lax.axis_size("mp"), lax.axis_size("dp")
    examples, emb = pooled.shape
    hid = delta.shape[1]
    width = row_ids.shape[-1]
    cap = width // owners
    slots = lookup_slot[:, 0, :].T
    looks = slots.shape[0]
    counts, ids = send_counts[0], row_ids[0]
    half, part = emb // 2, emb // 8
    tail = -(-cap // (8 * emb)) * 8

    xgrad, delta, pooled, slots, partial = call(
        first_kernel,
        [((emb, examples), F32), (delta.shape, BF16), (pooled.shape, BF16), (slots.shape, I32)]
        + [((2, examples), F32)],
        2 * emb * examples * hid,
        *[pltpu.with_memory_space_constraint(a, pltpu.HBM) for a in (delta, w_first, pooled, slots)],
        specs=[HBM] * 4,
        scratch=[pltpu.VMEM(w_first.shape, BF16), pltpu.SemaphoreType.DMA((3 + examples // CHUNK,))],
    )
    norms = [lax.ppermute(partial, "mp", r) for r in rounds(owners)]
    named, turned, targets, delta_sq = call(
        functools.partial(named_kernel, owners),
        [((width, examples), BF16), ((emb, examples), F32), ((owners, 1, cap), F32)]
        + [((1, examples), F32)],
        8 * width * examples * looks, counts, slots, pooled, ids, delta,
        specs=[SMEM, VMEM, VMEM, VMEM, VMEM],
    )
    clip, scaled, theirs = call(
        clip_kernel,
        [((1, examples), F32), ((half, examples), BF16), ((half, hid), F32)],
        2 * half * examples * hid,
        *norms, partial, turned, delta_sq, delta, named,
        specs=[VMEM] * (len(norms) + 4) + [ANY],
        scratch=[pltpu.VMEM((emb, examples), F32)],
    )
    steps = pairings(owners)
    swap = [(i, i ^ 1) for i in range(n_dp)]
    came = lax.ppermute(theirs, "dp", swap)
    (mine,) = call(mine_kernel, [((half, hid), F32)], 2 * half * examples * hid, scaled, delta)

    def chips(piece, s):
        return lax.ppermute(piece, "dp", [(i, i ^ (2 * s)) for i in range(n_dp)])

    hops = (0, 2, 3, 1)
    if n_dp == 8:
        parts = call(
            functools.partial(split_kernel, hops), [((part, hid), F32)] * 4, half * hid, mine, came
        )
    else:
        parts = [mine + came]
    unique = call(
        functools.partial(unique_kernel, owners), [((cap + tail, emb), F32)] * owners,
        4 * width * examples * emb, named, xgrad, clip, targets, parts[0], specs=[VMEM] * 4 + [ANY],
    )
    for s in range(1, owners):
        unique[s] = lax.ppermute(unique[s], "mp", steps[s - 1])
    if n_dp == 8:
        got = [chips(piece, s) for piece, s in zip(parts[1:], hops[1:])]
        got, unique[0] = lax.optimization_barrier((got, unique[0]))
        total = parts[0] + got[0] + got[1] + got[2]
        order = (0, 3, 2, 1)
        own = [total] + [chips(total, s) for s in order[1:]]
        own[0], *unique = lax.optimization_barrier((own[0], *unique))
        near = jnp.concatenate(own[:2])
        ends = [lax.ppermute(half_of, "dp", swap) for half_of in (near, jnp.concatenate(own[2:]))]
    else:
        groups = [list(range(c, n_dp, 2)) for c in (0, 1)]
        order = (0,)
        own = [lax.psum(parts[0], "dp", axis_index_groups=groups)]
        ends = [lax.ppermute(own[0], "dp", swap)]
    writes = len(own) + len(own) // 2
    table_grad, dense_grad = call(
        functools.partial(place_kernel, owners, cap, order),
        [((owners, ROWS_DEV, emb), F32), ((emb, hid), F32)],
        4 * owners * ROWS_DEV * cap * emb, *unique, *own, *ends[:-1], out_specs=[HBM, HBM],
        scratch=[pltpu.VMEM((owners, ROWS_DEV, emb), F32), pltpu.SemaphoreType.DMA((owners + writes,))],
    )
    rest = order[len(order) // 2:]
    (dense_grad,) = call(
        functools.partial(finish_kernel, rest), [((emb, hid), F32)], 0, dense_grad, ends[-1],
        specs=[HBM, VMEM], out_specs=[HBM], scratch=[pltpu.SemaphoreType.DMA((len(rest),))],
        aliases={0: 0},
    )
    return (dense_grad, table_grad[None])


def solution(mesh):
    placed = (
        P("dp", "mp"),
        P("dp", None),
        P("mp", None),
        P("dp", "mp", None),
        P("dp", "mp", None),
        P("dp", "mp", None),
    )
    return jax.shard_map(
        on_device,
        mesh=mesh,
        in_specs=placed,
        out_specs=(P("mp", None), P("dp", None, "mp", None)),
        check_vma=False,
    )
```

```python
import functools

import jax
import jax.numpy as jnp
from jax import lax
from jax.experimental import pallas as pl
from jax.experimental.pallas import tpu as pltpu
from jax.sharding import PartitionSpec as P

ROWS_DEV = 512
CLIP_NORM = 8.0
EPSILON = 1e-06

VMEM = pl.BlockSpec(memory_space=pltpu.VMEM)
SMEM = pl.BlockSpec(memory_space=pltpu.SMEM)
HBM = pl.BlockSpec(memory_space=pltpu.HBM)
ANY = pl.BlockSpec(memory_space=pl.ANY)
CHUNK = 512
F32, BF16, I32 = jnp.float32, jnp.bfloat16, jnp.int32


def pairings(n):
    if n & (n - 1) == 0:
        return [[(i, i ^ s) for i in range(n)] for s in range(1, n)]
    return [[(i, (i + s) % n) for i in range(n)] for s in range(1, n)]


def rounds(n):
    return pairings(n)


def peer_to(me, s, n):
    return me ^ s if n & (n - 1) == 0 else lax.rem(me + s, n)


def peer_from(me, s, n):
    return me ^ s if n & (n - 1) == 0 else lax.rem(me + n - s, n)


def call(kernel, outs, flops, *args, specs=None, out_specs=None, scratch=(), aliases=None):
    size = sum(a.size * a.dtype.itemsize for a in args)
    return list(pl.pallas_call(
        kernel,
        out_shape=[jax.ShapeDtypeStruct(shape, dtype) for shape, dtype in outs],
        in_specs=specs or [VMEM] * len(args),
        out_specs=out_specs or [VMEM] * len(outs),
        scratch_shapes=list(scratch),
        input_output_aliases=aliases or {},
        compiler_params=pltpu.CompilerParams(vmem_limit_bytes=16 * 2**20),
        cost_estimate=pl.CostEstimate(flops=flops, bytes_accessed=size, transcendentals=0),
    )(*args))


def window(counts_ref, me, s, owners):
    owner = peer_to(me, s, owners)
    start, count = jnp.int32(0), jnp.int32(0)
    for o in range(owners):
        here = counts_ref[0, o]
        start = start + jnp.where(o < owner, here, 0)
        count = count + jnp.where(o == owner, here, 0)
    return start, count


def first_kernel(delta_hbm, w_hbm, pooled_hbm, slots_hbm, *refs):
    xgrad_ref, delta_ref, pooled_ref, slots_ref, partial_ref, w_ref, sems = refs
    examples, emb = pooled_ref.shape
    looks = slots_ref.shape[0]
    blocks = list(range(0, examples, CHUNK))
    pairs = [(w_hbm, w_ref)]
    pairs += [(delta_hbm.at[pl.ds(r, CHUNK)], delta_ref.at[pl.ds(r, CHUNK)]) for r in blocks]
    pairs += [(slots_hbm, slots_ref), (pooled_hbm, pooled_ref)]
    copies = [pltpu.make_async_copy(a, b, sems.at[i]) for i, (a, b) in enumerate(pairs)]
    for copy in copies[-2:] + copies[:-2]:
        copy.start()
    n = len(blocks)
    for copy in copies[1 + n:]:
        copy.wait()
    slots = slots_ref[...]
    same = jnp.full(slots.shape, 1.0, F32)
    for shift in range(1, looks):
        same = same + jnp.where(slots == pltpu.roll(slots, shift, 0), 1.0, 0.0)
    repeats = jnp.sum(same, axis=0, keepdims=True)
    copies[0].wait()
    norms = []
    for i, r in enumerate(blocks):
        copies[1 + i].wait()
        xgrad = lax.dot_general(
            w_ref[...], delta_ref[r:r + CHUNK, :], (((1,), (1,)), ((), ())),
            preferred_element_type=F32,
        )
        xgrad_ref[:, r:r + CHUNK] = xgrad
        norms.append(jnp.sum(xgrad * xgrad, axis=0, keepdims=True))
    for i, r in enumerate(blocks):
        sums = []
        for q in range(r, r + CHUNK, 128):
            piece = pooled_ref[q:q + 128, :].astype(F32)
            sums.append(jnp.sum((piece * piece).T, axis=0, keepdims=True))
        partial_ref[0:1, r:r + CHUNK] = jnp.concatenate(sums, axis=1)
        partial_ref[1:2, r:r + CHUNK] = repeats[:, r:r + CHUNK] * norms[i]


def named_kernel(owners, counts_ref, slots_ref, pooled_ref, ids_ref, delta_ref, named_ref, turned_ref, targets_ref, delta_sq_ref):
    for r in range(0, delta_ref.shape[0], 128):
        total = jnp.zeros((128, 128), F32)
        for c in range(0, delta_ref.shape[1], 128):
            piece = delta_ref[r:r + 128, c:c + 128].astype(F32)
            total = total + piece * piece
        delta_sq_ref[:, r:r + 128] = jnp.sum(total.T, axis=0, keepdims=True)
    turned_ref[...] = pooled_ref[...].astype(F32).T
    width = named_ref.shape[0]
    ids = jnp.broadcast_to(ids_ref[...], (8, width))
    looks, examples = slots_ref.shape
    cap = width // owners
    me = lax.axis_index("mp")
    one, zero = jnp.ones((16, 128), BF16), jnp.zeros((16, 128), BF16)
    wide = {}
    for l in range(looks):
        for c in range(0, examples, 128):
            line = jnp.broadcast_to(slots_ref[l:l + 1, c:c + 128], (16, 128))
            wide[l, c // 128] = line.astype(jnp.int16)
    for s in range(owners):
        start, count = window(counts_ref, me, s, owners)
        mine = pltpu.roll(ids, lax.rem(width - start, width), 1)[0:1, :cap]
        inside = lax.broadcasted_iota(I32, (1, cap), 1) < count
        targets_ref[s] = jnp.where(inside, mine, -1).astype(F32)
        for r in range(0, cap, 16):
            place = lax.broadcasted_iota(I32, (16, 128), 0) + r
            name = jnp.where(place < count, place + start, -1).astype(jnp.int16)
            for c in range(0, examples, 128):
                total = jnp.zeros((16, 128), BF16)
                for l in range(looks):
                    total = total + jnp.where(wide[l, c // 128] == name, one, zero)
                named_ref[s * cap + r:s * cap + r + 16, c:c + 128] = total


def clip_kernel(*refs):
    *messages, turned_ref, delta_sq_ref, delta_ref, _, clip_ref, scaled_ref, theirs_ref, wide_ref = refs
    half = theirs_ref.shape[0]
    core = lax.rem(lax.axis_index("dp"), 2)
    total = messages[0][...]
    for message in messages[1:]:
        total = total + message[...]
    norm_sq = delta_sq_ref[...] * total[0:1, :] + total[1:2, :]
    clip = jnp.minimum(1.0, CLIP_NORM / jnp.sqrt(norm_sq + EPSILON))
    clip_ref[...] = clip
    wide_ref[...] = turned_ref[...] * clip
    other = wide_ref[pl.ds((1 - core) * half, half), :].astype(BF16)
    theirs_ref[...] = jnp.dot(other, delta_ref[...], preferred_element_type=F32)
    scaled_ref[...] = wide_ref[pl.ds(core * half, half), :].astype(BF16)


def mine_kernel(scaled_ref, delta_ref, mine_ref):
    mine_ref[...] = jnp.dot(scaled_ref[...], delta_ref[...], preferred_element_type=F32)


def split_kernel(steps, mine_ref, came_ref, _, *part_refs):
    part = part_refs[0].shape[0]
    chip = lax.axis_index("dp") // 2
    for step, out_ref in zip(steps, part_refs):
        rows = pl.ds((chip ^ step) * part, part)
        out_ref[...] = mine_ref[rows, :] + came_ref[rows, :]


def unique_kernel(owners, named_ref, xgrad_ref, clip_ref, targets_ref, _, *out_refs):
    emb = xgrad_ref.shape[0]
    cap = named_ref.shape[0] // owners
    wide = xgrad_ref[...] * clip_ref[...]
    hi = wide.astype(BF16)
    lo = (wide - hi.astype(F32)).astype(BF16)
    terms = jnp.concatenate([hi, lo], axis=0)
    for s in range(owners):
        both = lax.dot_general(
            named_ref[s * cap:(s + 1) * cap, :], terms, (((1,), (1,)), ((), ())),
            preferred_element_type=F32,
        )
        out_refs[s][:cap, :] = both[:, :emb] + both[:, emb:]
        out_refs[s][cap:, :] = jnp.zeros((out_refs[s].shape[0] - cap, emb), F32)
        for q in range(cap // emb):
            out_refs[s][cap + q:cap + q + 1, :] = targets_ref[s, :, q * emb:(q + 1) * emb]


def place_of(hop, flip, rows, part):
    me = lax.axis_index("dp")
    chip, core = me // 2, lax.rem(me, 2)
    core = 1 - core if flip else core
    return pl.ds(core * (rows // 2) + ((chip ^ hop) * part if 2 * part < rows else 0), part)


def place_kernel(owners, cap, order, *refs):
    pieces = refs[:owners]
    own, ends = refs[owners:owners + len(order)], refs[owners + len(order):-4]
    table_ref, dense_ref, rows_ref, sems = refs[-4:]
    emb = pieces[0].shape[1]
    part = own[0].shape[0]
    me = lax.axis_index("mp")
    places = [(own[i], hop, 0) for i, hop in enumerate(order)]
    for end in ends:
        places += [(end.at[pl.ds(i * part, part)], hop, 1) for i, hop in enumerate(order[:len(order) // 2])]
    copies = []
    for i, (piece, hop, flip) in enumerate(places):
        rows = place_of(hop, flip, dense_ref.shape[0], part)
        copies.append(pltpu.make_async_copy(piece, dense_ref.at[rows], sems.at[owners + i]))
        copies[-1].start()
    row = lax.broadcasted_iota(I32, (ROWS_DEV, cap), 0).astype(F32)
    for s in range(owners):
        ids = [pieces[s][cap + q:cap + q + 1, :] for q in range(cap // emb)]
        ids = jnp.concatenate(ids, axis=1)
        hot = jnp.where(row == ids, 1.0, 0.0).astype(BF16)
        wide = pieces[s][:cap, :]
        hi = wide.astype(BF16)
        lo = (wide - hi.astype(F32)).astype(BF16)
        both = jnp.dot(hot, jnp.concatenate([hi, lo], axis=1), preferred_element_type=F32)
        rows_ref[s] = both[:, :emb] + both[:, emb:]
        copy = pltpu.make_async_copy(
            rows_ref.at[s], table_ref.at[peer_from(me, s, owners)], sems.at[s]
        )
        copy.start()
        copies.append(copy)
    for copy in copies:
        copy.wait()


def finish_kernel(order, _, end_ref, dense_ref, sems):
    part = end_ref.shape[0] // len(order)
    copies = []
    for i, hop in enumerate(order):
        rows = place_of(hop, 1, dense_ref.shape[0], part)
        copies.append(pltpu.make_async_copy(end_ref.at[pl.ds(i * part, part)], dense_ref.at[rows], sems.at[i]))
        copies[-1].start()
    for copy in copies:
        copy.wait()


def on_device(pooled, delta, w_first, lookup_slot, row_ids, send_counts):
    owners, n_dp = lax.axis_size("mp"), lax.axis_size("dp")
    examples, emb = pooled.shape
    hid = delta.shape[1]
    width = row_ids.shape[-1]
    cap = width // owners
    slots = lookup_slot[:, 0, :].T
    looks = slots.shape[0]
    counts, ids = send_counts[0], row_ids[0]
    half, part = emb // 2, emb // 8
    tail = -(-cap // (8 * emb)) * 8

    xgrad, delta, pooled, slots, partial = call(
        first_kernel,
        [((emb, examples), F32), (delta.shape, BF16), (pooled.shape, BF16), (slots.shape, I32)]
        + [((2, examples), F32)],
        2 * emb * examples * hid,
        *[pltpu.with_memory_space_constraint(a, pltpu.HBM) for a in (delta, w_first, pooled, slots)],
        specs=[HBM] * 4,
        scratch=[pltpu.VMEM(w_first.shape, BF16), pltpu.SemaphoreType.DMA((3 + examples // CHUNK,))],
    )
    norms = [lax.ppermute(partial, "mp", r) for r in rounds(owners)]
    named, turned, targets, delta_sq = call(
        functools.partial(named_kernel, owners),
        [((width, examples), BF16), ((emb, examples), F32), ((owners, 1, cap), F32)]
        + [((1, examples), F32)],
        8 * width * examples * looks, counts, slots, pooled, ids, delta,
        specs=[SMEM, VMEM, VMEM, VMEM, VMEM],
    )
    clip, scaled, theirs = call(
        clip_kernel,
        [((1, examples), F32), ((half, examples), BF16), ((half, hid), F32)],
        2 * half * examples * hid,
        *norms, partial, turned, delta_sq, delta, named,
        specs=[VMEM] * (len(norms) + 4) + [ANY],
        scratch=[pltpu.VMEM((emb, examples), F32)],
    )
    steps = pairings(owners)
    swap = [(i, i ^ 1) for i in range(n_dp)]
    came = lax.ppermute(theirs, "dp", swap)
    (mine,) = call(mine_kernel, [((half, hid), F32)], 2 * half * examples * hid, scaled, delta)

    def chips(piece, s):
        return lax.ppermute(piece, "dp", [(i, i ^ (2 * s)) for i in range(n_dp)])

    unique = call(
        functools.partial(unique_kernel, owners), [((cap + tail, emb), F32)] * owners,
        4 * width * examples * emb, named, xgrad, clip, targets, mine, specs=[VMEM] * 4 + [ANY],
    )
    hops = (0, 2, 3, 1)
    if n_dp == 8:
        parts = call(
            functools.partial(split_kernel, hops), [((part, hid), F32)] * 4, half * hid, mine, came,
            unique[0], specs=[VMEM, VMEM, ANY],
        )
    else:
        parts = [mine + came]
    for s in range(1, owners):
        unique[s] = lax.ppermute(unique[s], "mp", steps[s - 1])
    if n_dp == 8:
        got = [chips(piece, s) for piece, s in zip(parts[1:], hops[1:])]
        got, unique[0] = lax.optimization_barrier((got, unique[0]))
        total = parts[0] + got[0] + got[1] + got[2]
        order = (0, 3, 2, 1)
        own = [total] + [chips(total, s) for s in order[1:]]
        own[0], *unique = lax.optimization_barrier((own[0], *unique))
        near = jnp.concatenate(own[:2])
        ends = [lax.ppermute(half_of, "dp", swap) for half_of in (near, jnp.concatenate(own[2:]))]
    else:
        groups = [list(range(c, n_dp, 2)) for c in (0, 1)]
        order = (0,)
        own = [lax.psum(parts[0], "dp", axis_index_groups=groups)]
        ends = [lax.ppermute(own[0], "dp", swap)]
    writes = len(own) + len(own) // 2
    table_grad, dense_grad = call(
        functools.partial(place_kernel, owners, cap, order),
        [((owners, ROWS_DEV, emb), F32), ((emb, hid), F32)],
        4 * owners * ROWS_DEV * cap * emb, *unique, *own, *ends[:-1], out_specs=[HBM, HBM],
        scratch=[pltpu.VMEM((owners, ROWS_DEV, emb), F32), pltpu.SemaphoreType.DMA((owners + writes,))],
    )
    rest = order[len(order) // 2:]
    (dense_grad,) = call(
        functools.partial(finish_kernel, rest), [((emb, hid), F32)], 0, dense_grad, ends[-1],
        specs=[HBM, VMEM], out_specs=[HBM], scratch=[pltpu.SemaphoreType.DMA((len(rest),))],
        aliases={0: 0},
    )
    return (dense_grad, table_grad[None])


def solution(mesh):
    placed = (
        P("dp", "mp"),
        P("dp", None),
        P("mp", None),
        P("dp", "mp", None),
        P("dp", "mp", None),
        P("dp", "mp", None),
    )
    return jax.shard_map(
        on_device,
        mesh=mesh,
        in_specs=placed,
        out_specs=(P("mp", None), P("dp", None, "mp", None)),
        check_vma=False,
    )
```

```python
import functools

import jax
import jax.numpy as jnp
from jax import lax
from jax.experimental import pallas as pl
from jax.experimental.pallas import tpu as pltpu
from jax.sharding import PartitionSpec as P

ROWS_DEV = 512
CLIP_NORM = 8.0
EPSILON = 1e-06

VMEM = pl.BlockSpec(memory_space=pltpu.VMEM)
SMEM = pl.BlockSpec(memory_space=pltpu.SMEM)
HBM = pl.BlockSpec(memory_space=pltpu.HBM)
ANY = pl.BlockSpec(memory_space=pl.ANY)
CHUNK = 512
F32, BF16, I32 = jnp.float32, jnp.bfloat16, jnp.int32


def pairings(n):
    if n & (n - 1) == 0:
        return [[(i, i ^ s) for i in range(n)] for s in range(1, n)]
    return [[(i, (i + s) % n) for i in range(n)] for s in range(1, n)]


def rounds(n):
    return pairings(n)


def peer_to(me, s, n):
    return me ^ s if n & (n - 1) == 0 else lax.rem(me + s, n)


def peer_from(me, s, n):
    return me ^ s if n & (n - 1) == 0 else lax.rem(me + n - s, n)


def call(kernel, outs, flops, *args, specs=None, out_specs=None, scratch=(), aliases=None):
    size = sum(a.size * a.dtype.itemsize for a in args)
    return list(pl.pallas_call(
        kernel,
        out_shape=[jax.ShapeDtypeStruct(shape, dtype) for shape, dtype in outs],
        in_specs=specs or [VMEM] * len(args),
        out_specs=out_specs or [VMEM] * len(outs),
        scratch_shapes=list(scratch),
        input_output_aliases=aliases or {},
        compiler_params=pltpu.CompilerParams(vmem_limit_bytes=16 * 2**20),
        cost_estimate=pl.CostEstimate(flops=flops, bytes_accessed=size, transcendentals=0),
    )(*args))


def window(counts_ref, me, s, owners):
    owner = peer_to(me, s, owners)
    start, count = jnp.int32(0), jnp.int32(0)
    for o in range(owners):
        here = counts_ref[0, o]
        start = start + jnp.where(o < owner, here, 0)
        count = count + jnp.where(o == owner, here, 0)
    return start, count


def first_kernel(delta_hbm, w_hbm, pooled_hbm, slots_hbm, *refs):
    xgrad_ref, delta_ref, pooled_ref, slots_ref, partial_ref, w_ref, sems = refs
    examples, emb = pooled_ref.shape
    looks = slots_ref.shape[0]
    blocks = list(range(0, examples, CHUNK))
    pairs = [(w_hbm, w_ref)]
    pairs += [(delta_hbm.at[pl.ds(r, CHUNK)], delta_ref.at[pl.ds(r, CHUNK)]) for r in blocks]
    pairs += [(slots_hbm, slots_ref), (pooled_hbm, pooled_ref)]
    copies = [pltpu.make_async_copy(a, b, sems.at[i]) for i, (a, b) in enumerate(pairs)]
    for copy in copies[-2:] + copies[:-2]:
        copy.start()
    n = len(blocks)
    for copy in copies[1 + n:]:
        copy.wait()
    slots = slots_ref[...]
    same = jnp.full(slots.shape, 1.0, F32)
    for shift in range(1, looks):
        same = same + jnp.where(slots == pltpu.roll(slots, shift, 0), 1.0, 0.0)
    repeats = jnp.sum(same, axis=0, keepdims=True)
    for q in range(0, examples, 128):
        piece = pooled_ref[q:q + 128, :].astype(F32)
        partial_ref[0:1, q:q + 128] = jnp.sum((piece * piece).T, axis=0, keepdims=True)
    copies[0].wait()
    norms = []
    for i, r in enumerate(blocks):
        copies[1 + i].wait()
        xgrad = lax.dot_general(
            w_ref[...], delta_ref[r:r + CHUNK, :], (((1,), (1,)), ((), ())),
            preferred_element_type=F32,
        )
        xgrad_ref[:, r:r + CHUNK] = xgrad
        norms.append(jnp.sum(xgrad * xgrad, axis=0, keepdims=True))
    for i, r in enumerate(blocks):
        partial_ref[1:2, r:r + CHUNK] = repeats[:, r:r + CHUNK] * norms[i]


def named_kernel(owners, counts_ref, slots_ref, pooled_ref, ids_ref, delta_ref, named_ref, turned_ref, targets_ref, delta_sq_ref):
    for r in range(0, delta_ref.shape[0], 128):
        total = jnp.zeros((128, 128), F32)
        for c in range(0, delta_ref.shape[1], 128):
            piece = delta_ref[r:r + 128, c:c + 128].astype(F32)
            total = total + piece * piece
        delta_sq_ref[:, r:r + 128] = jnp.sum(total.T, axis=0, keepdims=True)
    turned_ref[...] = pooled_ref[...].astype(F32).T
    width = named_ref.shape[0]
    ids = jnp.broadcast_to(ids_ref[...], (8, width))
    looks, examples = slots_ref.shape
    cap = width // owners
    me = lax.axis_index("mp")
    one, zero = jnp.ones((16, 128), BF16), jnp.zeros((16, 128), BF16)
    wide = {}
    for l in range(looks):
        for c in range(0, examples, 128):
            line = jnp.broadcast_to(slots_ref[l:l + 1, c:c + 128], (16, 128))
            wide[l, c // 128] = line.astype(jnp.int16)
    for s in range(owners):
        start, count = window(counts_ref, me, s, owners)
        mine = pltpu.roll(ids, lax.rem(width - start, width), 1)[0:1, :cap]
        inside = lax.broadcasted_iota(I32, (1, cap), 1) < count
        targets_ref[s] = jnp.where(inside, mine, -1).astype(F32)
        for r in range(0, cap, 16):
            place = lax.broadcasted_iota(I32, (16, 128), 0) + r
            name = jnp.where(place < count, place + start, -1).astype(jnp.int16)
            for c in range(0, examples, 128):
                total = jnp.zeros((16, 128), BF16)
                for l in range(looks):
                    total = total + jnp.where(wide[l, c // 128] == name, one, zero)
                named_ref[s * cap + r:s * cap + r + 16, c:c + 128] = total


def clip_kernel(*refs):
    *messages, turned_ref, delta_sq_ref, delta_ref, _, clip_ref, scaled_ref, theirs_ref, wide_ref = refs
    half = theirs_ref.shape[0]
    core = lax.rem(lax.axis_index("dp"), 2)
    total = messages[0][...]
    for message in messages[1:]:
        total = total + message[...]
    norm_sq = delta_sq_ref[...] * total[0:1, :] + total[1:2, :]
    clip = jnp.minimum(1.0, CLIP_NORM / jnp.sqrt(norm_sq + EPSILON))
    clip_ref[...] = clip
    wide_ref[...] = turned_ref[...] * clip
    other = wide_ref[pl.ds((1 - core) * half, half), :].astype(BF16)
    theirs_ref[...] = jnp.dot(other, delta_ref[...], preferred_element_type=F32)
    scaled_ref[...] = wide_ref[pl.ds(core * half, half), :].astype(BF16)


def mine_kernel(scaled_ref, delta_ref, mine_ref):
    mine_ref[...] = jnp.dot(scaled_ref[...], delta_ref[...], preferred_element_type=F32)


def split_kernel(steps, mine_ref, came_ref, _, *part_refs):
    part = part_refs[0].shape[0]
    chip = lax.axis_index("dp") // 2
    for step, out_ref in zip(steps, part_refs):
        rows = pl.ds((chip ^ step) * part, part)
        out_ref[...] = mine_ref[rows, :] + came_ref[rows, :]


def unique_kernel(owners, named_ref, xgrad_ref, clip_ref, targets_ref, _, *out_refs):
    emb = xgrad_ref.shape[0]
    cap = named_ref.shape[0] // owners
    wide = xgrad_ref[...] * clip_ref[...]
    hi = wide.astype(BF16)
    lo = (wide - hi.astype(F32)).astype(BF16)
    terms = jnp.concatenate([hi, lo], axis=0)
    for s in range(owners):
        both = lax.dot_general(
            named_ref[s * cap:(s + 1) * cap, :], terms, (((1,), (1,)), ((), ())),
            preferred_element_type=F32,
        )
        out_refs[s][:cap, :] = both[:, :emb] + both[:, emb:]
        out_refs[s][cap:, :] = jnp.zeros((out_refs[s].shape[0] - cap, emb), F32)
        for q in range(cap // emb):
            out_refs[s][cap + q:cap + q + 1, :] = targets_ref[s, :, q * emb:(q + 1) * emb]


def place_of(hop, flip, rows, part):
    me = lax.axis_index("dp")
    chip, core = me // 2, lax.rem(me, 2)
    core = 1 - core if flip else core
    return pl.ds(core * (rows // 2) + ((chip ^ hop) * part if 2 * part < rows else 0), part)


def place_kernel(owners, cap, order, *refs):
    pieces = refs[:owners]
    own, ends = refs[owners:owners + len(order)], refs[owners + len(order):-4]
    table_ref, dense_ref, rows_ref, sems = refs[-4:]
    emb = pieces[0].shape[1]
    part = own[0].shape[0]
    me = lax.axis_index("mp")
    places = [(own[i], hop, 0) for i, hop in enumerate(order)]
    for end in ends:
        places += [(end.at[pl.ds(i * part, part)], hop, 1) for i, hop in enumerate(order[:len(order) // 2])]
    copies = []
    for i, (piece, hop, flip) in enumerate(places):
        rows = place_of(hop, flip, dense_ref.shape[0], part)
        copies.append(pltpu.make_async_copy(piece, dense_ref.at[rows], sems.at[owners + i]))
        copies[-1].start()
    row = lax.broadcasted_iota(I32, (ROWS_DEV, cap), 0).astype(F32)
    for s in range(owners):
        ids = [pieces[s][cap + q:cap + q + 1, :] for q in range(cap // emb)]
        ids = jnp.concatenate(ids, axis=1)
        hot = jnp.where(row == ids, 1.0, 0.0).astype(BF16)
        wide = pieces[s][:cap, :]
        hi = wide.astype(BF16)
        lo = (wide - hi.astype(F32)).astype(BF16)
        both = jnp.dot(hot, jnp.concatenate([hi, lo], axis=1), preferred_element_type=F32)
        rows_ref[s] = both[:, :emb] + both[:, emb:]
        copy = pltpu.make_async_copy(
            rows_ref.at[s], table_ref.at[peer_from(me, s, owners)], sems.at[s]
        )
        copy.start()
        copies.append(copy)
    for copy in copies:
        copy.wait()


def finish_kernel(order, _, end_ref, dense_ref, sems):
    part = end_ref.shape[0] // len(order)
    copies = []
    for i, hop in enumerate(order):
        rows = place_of(hop, 1, dense_ref.shape[0], part)
        copies.append(pltpu.make_async_copy(end_ref.at[pl.ds(i * part, part)], dense_ref.at[rows], sems.at[i]))
        copies[-1].start()
    for copy in copies:
        copy.wait()


def on_device(pooled, delta, w_first, lookup_slot, row_ids, send_counts):
    owners, n_dp = lax.axis_size("mp"), lax.axis_size("dp")
    examples, emb = pooled.shape
    hid = delta.shape[1]
    width = row_ids.shape[-1]
    cap = width // owners
    slots = lookup_slot[:, 0, :].T
    looks = slots.shape[0]
    counts, ids = send_counts[0], row_ids[0]
    half, part = emb // 2, emb // 8
    tail = -(-cap // (8 * emb)) * 8

    xgrad, delta, pooled, slots, partial = call(
        first_kernel,
        [((emb, examples), F32), (delta.shape, BF16), (pooled.shape, BF16), (slots.shape, I32)]
        + [((2, examples), F32)],
        2 * emb * examples * hid,
        *[pltpu.with_memory_space_constraint(a, pltpu.HBM) for a in (delta, w_first, pooled, slots)],
        specs=[HBM] * 4,
        scratch=[pltpu.VMEM(w_first.shape, BF16), pltpu.SemaphoreType.DMA((3 + examples // CHUNK,))],
    )
    norms = [lax.ppermute(partial, "mp", r) for r in rounds(owners)]
    named, turned, targets, delta_sq = call(
        functools.partial(named_kernel, owners),
        [((width, examples), BF16), ((emb, examples), F32), ((owners, 1, cap), F32)]
        + [((1, examples), F32)],
        8 * width * examples * looks, counts, slots, pooled, ids, delta,
        specs=[SMEM, VMEM, VMEM, VMEM, VMEM],
    )
    clip, scaled, theirs = call(
        clip_kernel,
        [((1, examples), F32), ((half, examples), BF16), ((half, hid), F32)],
        2 * half * examples * hid,
        *norms, partial, turned, delta_sq, delta, named,
        specs=[VMEM] * (len(norms) + 4) + [ANY],
        scratch=[pltpu.VMEM((emb, examples), F32)],
    )
    steps = pairings(owners)
    swap = [(i, i ^ 1) for i in range(n_dp)]
    came = lax.ppermute(theirs, "dp", swap)
    (mine,) = call(mine_kernel, [((half, hid), F32)], 2 * half * examples * hid, scaled, delta)

    def chips(piece, s):
        return lax.ppermute(piece, "dp", [(i, i ^ (2 * s)) for i in range(n_dp)])

    unique = call(
        functools.partial(unique_kernel, owners), [((cap + tail, emb), F32)] * owners,
        4 * width * examples * emb, named, xgrad, clip, targets, mine, specs=[VMEM] * 4 + [ANY],
    )
    hops = (0, 2, 3, 1)
    if n_dp == 8:
        parts = call(
            functools.partial(split_kernel, hops), [((part, hid), F32)] * 4, half * hid, mine, came,
            unique[0], specs=[VMEM, VMEM, ANY],
        )
    else:
        parts = [mine + came]
    for s in range(1, owners):
        unique[s] = lax.ppermute(unique[s], "mp", steps[s - 1])
    if n_dp == 8:
        got = [chips(piece, s) for piece, s in zip(parts[1:], hops[1:])]
        got, unique[0] = lax.optimization_barrier((got, unique[0]))
        total = parts[0] + got[0] + got[1] + got[2]
        order = (0, 3, 2, 1)
        own = [total] + [chips(total, s) for s in order[1:]]
        own[0], *unique = lax.optimization_barrier((own[0], *unique))
        near = jnp.concatenate(own[:2])
        ends = [lax.ppermute(half_of, "dp", swap) for half_of in (near, jnp.concatenate(own[2:]))]
    else:
        groups = [list(range(c, n_dp, 2)) for c in (0, 1)]
        order = (0,)
        own = [lax.psum(parts[0], "dp", axis_index_groups=groups)]
        ends = [lax.ppermute(own[0], "dp", swap)]
    writes = len(own) + len(own) // 2
    table_grad, dense_grad = call(
        functools.partial(place_kernel, owners, cap, order),
        [((owners, ROWS_DEV, emb), F32), ((emb, hid), F32)],
        4 * owners * ROWS_DEV * cap * emb, *unique, *own, *ends[:-1], out_specs=[HBM, HBM],
        scratch=[pltpu.VMEM((owners, ROWS_DEV, emb), F32), pltpu.SemaphoreType.DMA((owners + writes,))],
    )
    rest = order[len(order) // 2:]
    (dense_grad,) = call(
        functools.partial(finish_kernel, rest), [((emb, hid), F32)], 0, dense_grad, ends[-1],
        specs=[HBM, VMEM], out_specs=[HBM], scratch=[pltpu.SemaphoreType.DMA((len(rest),))],
        aliases={0: 0},
    )
    return (dense_grad, table_grad[None])


def solution(mesh):
    placed = (
        P("dp", "mp"),
        P("dp", None),
        P("mp", None),
        P("dp", "mp", None),
        P("dp", "mp", None),
        P("dp", "mp", None),
    )
    return jax.shard_map(
        on_device,
        mesh=mesh,
        in_specs=placed,
        out_specs=(P("mp", None), P("dp", None, "mp", None)),
        check_vma=False,
    )
```

```python
import functools

import jax
import jax.numpy as jnp
from jax import lax
from jax.experimental import pallas as pl
from jax.experimental.pallas import tpu as pltpu
from jax.sharding import PartitionSpec as P

ROWS_DEV = 512
CLIP_NORM = 8.0
EPSILON = 1e-06

VMEM = pl.BlockSpec(memory_space=pltpu.VMEM)
SMEM = pl.BlockSpec(memory_space=pltpu.SMEM)
HBM = pl.BlockSpec(memory_space=pltpu.HBM)
ANY = pl.BlockSpec(memory_space=pl.ANY)
CHUNK = 512
F32, BF16, I32 = jnp.float32, jnp.bfloat16, jnp.int32


def pairings(n):
    if n & (n - 1) == 0:
        return [[(i, i ^ s) for i in range(n)] for s in range(1, n)]
    return [[(i, (i + s) % n) for i in range(n)] for s in range(1, n)]


def rounds(n):
    return pairings(n)


def peer_to(me, s, n):
    return me ^ s if n & (n - 1) == 0 else lax.rem(me + s, n)


def peer_from(me, s, n):
    return me ^ s if n & (n - 1) == 0 else lax.rem(me + n - s, n)


def call(kernel, outs, flops, *args, specs=None, out_specs=None, scratch=(), aliases=None):
    size = sum(a.size * a.dtype.itemsize for a in args)
    return list(pl.pallas_call(
        kernel,
        out_shape=[jax.ShapeDtypeStruct(shape, dtype) for shape, dtype in outs],
        in_specs=specs or [VMEM] * len(args),
        out_specs=out_specs or [VMEM] * len(outs),
        scratch_shapes=list(scratch),
        input_output_aliases=aliases or {},
        compiler_params=pltpu.CompilerParams(vmem_limit_bytes=16 * 2**20),
        cost_estimate=pl.CostEstimate(flops=flops, bytes_accessed=size, transcendentals=0),
    )(*args))


def window(counts_ref, me, s, owners):
    owner = peer_to(me, s, owners)
    start, count = jnp.int32(0), jnp.int32(0)
    for o in range(owners):
        here = counts_ref[0, o]
        start = start + jnp.where(o < owner, here, 0)
        count = count + jnp.where(o == owner, here, 0)
    return start, count


def first_kernel(delta_hbm, w_hbm, pooled_hbm, slots_hbm, *refs):
    xgrad_ref, delta_ref, pooled_ref, slots_ref, partial_ref, w_ref, sems = refs
    examples, emb = pooled_ref.shape
    looks = slots_ref.shape[0]
    blocks = list(range(0, examples, CHUNK))
    pairs = [(w_hbm, w_ref)]
    pairs += [(delta_hbm.at[pl.ds(r, CHUNK)], delta_ref.at[pl.ds(r, CHUNK)]) for r in blocks]
    pairs += [(slots_hbm, slots_ref), (pooled_hbm, pooled_ref)]
    copies = [pltpu.make_async_copy(a, b, sems.at[i]) for i, (a, b) in enumerate(pairs)]
    for copy in copies[-2:] + copies[:-2]:
        copy.start()
    n = len(blocks)
    for copy in copies[1 + n:]:
        copy.wait()
    slots = slots_ref[...]
    same = jnp.full(slots.shape, 1.0, F32)
    for shift in range(1, looks):
        same = same + jnp.where(slots == pltpu.roll(slots, shift, 0), 1.0, 0.0)
    repeats = jnp.sum(same, axis=0, keepdims=True)
    copies[0].wait()
    norms = []
    for i, r in enumerate(blocks):
        copies[1 + i].wait()
        xgrad = lax.dot_general(
            w_ref[...], delta_ref[r:r + CHUNK, :], (((1,), (1,)), ((), ())),
            preferred_element_type=F32,
        )
        xgrad_ref[:, r:r + CHUNK] = xgrad
        norms.append(jnp.sum(xgrad * xgrad, axis=0, keepdims=True))
    for i, r in enumerate(blocks):
        sums = []
        for q in range(r, r + CHUNK, 128):
            piece = pooled_ref[q:q + 128, :].astype(F32)
            sums.append(jnp.sum((piece * piece).T, axis=0, keepdims=True))
        partial_ref[0:1, r:r + CHUNK] = jnp.concatenate(sums, axis=1)
        partial_ref[1:2, r:r + CHUNK] = repeats[:, r:r + CHUNK] * norms[i]


def named_kernel(owners, counts_ref, slots_ref, pooled_ref, ids_ref, delta_ref, named_ref, turned_ref, targets_ref, delta_sq_ref):
    for r in range(0, delta_ref.shape[0], 128):
        total = jnp.zeros((128, 128), F32)
        for c in range(0, delta_ref.shape[1], 128):
            piece = delta_ref[r:r + 128, c:c + 128].astype(F32)
            total = total + piece * piece
        delta_sq_ref[:, r:r + 128] = jnp.sum(total.T, axis=0, keepdims=True)
    turned_ref[...] = pooled_ref[...].astype(F32).T
    width = named_ref.shape[0]
    ids = jnp.broadcast_to(ids_ref[...], (8, width))
    looks, examples = slots_ref.shape
    cap = width // owners
    me = lax.axis_index("mp")
    one, zero = jnp.ones((16, 128), BF16), jnp.zeros((16, 128), BF16)
    wide = {}
    for l in range(looks):
        for c in range(0, examples, 128):
            line = jnp.broadcast_to(slots_ref[l:l + 1, c:c + 128], (16, 128))
            wide[l, c // 128] = line.astype(jnp.int16)
    for s in range(owners):
        start, count = window(counts_ref, me, s, owners)
        mine = pltpu.roll(ids, lax.rem(width - start, width), 1)[0:1, :cap]
        inside = lax.broadcasted_iota(I32, (1, cap), 1) < count
        targets_ref[s] = jnp.where(inside, mine, -1).astype(F32)
        for r in range(0, cap, 16):
            place = lax.broadcasted_iota(I32, (16, 128), 0) + r
            name = jnp.where(place < count, place + start, -1).astype(jnp.int16)
            for c in range(0, examples, 128):
                total = jnp.zeros((16, 128), BF16)
                for l in range(looks):
                    total = total + jnp.where(wide[l, c // 128] == name, one, zero)
                named_ref[s * cap + r:s * cap + r + 16, c:c + 128] = total


def clip_kernel(*refs):
    *messages, turned_ref, delta_sq_ref, delta_ref, _, clip_ref, scaled_ref, theirs_ref, wide_ref = refs
    half = theirs_ref.shape[0]
    core = lax.rem(lax.axis_index("dp"), 2)
    total = messages[0][...]
    for message in messages[1:]:
        total = total + message[...]
    norm_sq = delta_sq_ref[...] * total[0:1, :] + total[1:2, :]
    clip = jnp.minimum(1.0, CLIP_NORM / jnp.sqrt(norm_sq + EPSILON))
    clip_ref[...] = clip
    wide_ref[...] = turned_ref[...] * clip
    other = wide_ref[pl.ds((1 - core) * half, half), :].astype(BF16)
    theirs_ref[...] = jnp.dot(other, delta_ref[...], preferred_element_type=F32)
    scaled_ref[...] = wide_ref[pl.ds(core * half, half), :].astype(BF16)


def mine_kernel(scaled_ref, delta_ref, mine_ref):
    mine_ref[...] = jnp.dot(scaled_ref[...], delta_ref[...], preferred_element_type=F32)


def split_kernel(steps, mine_ref, came_ref, _, *part_refs):
    part = part_refs[0].shape[0]
    chip = lax.axis_index("dp") // 2
    for step, out_ref in zip(steps, part_refs):
        rows = pl.ds((chip ^ step) * part, part)
        out_ref[...] = mine_ref[rows, :] + came_ref[rows, :]


def unique_kernel(owners, named_ref, xgrad_ref, clip_ref, targets_ref, _, *out_refs):
    emb = xgrad_ref.shape[0]
    cap = named_ref.shape[0] // owners
    wide = xgrad_ref[...] * clip_ref[...]
    hi = wide.astype(BF16)
    lo = (wide - hi.astype(F32)).astype(BF16)
    terms = jnp.concatenate([hi, lo], axis=0)
    for s in range(owners):
        both = lax.dot_general(
            named_ref[s * cap:(s + 1) * cap, :], terms, (((1,), (1,)), ((), ())),
            preferred_element_type=F32,
        )
        out_refs[s][:cap, :] = both[:, :emb] + both[:, emb:]
        out_refs[s][cap:, :] = jnp.zeros((out_refs[s].shape[0] - cap, emb), F32)
        for q in range(cap // emb):
            out_refs[s][cap + q:cap + q + 1, :] = targets_ref[s, :, q * emb:(q + 1) * emb]


def place_of(hop, flip, rows, part):
    me = lax.axis_index("dp")
    chip, core = me // 2, lax.rem(me, 2)
    core = 1 - core if flip else core
    return pl.ds(core * (rows // 2) + ((chip ^ hop) * part if 2 * part < rows else 0), part)


def place_kernel(owners, cap, order, *refs):
    pieces = refs[:owners]
    own, ends = refs[owners:owners + len(order)], refs[owners + len(order):-4]
    table_ref, dense_ref, rows_ref, sems = refs[-4:]
    emb = pieces[0].shape[1]
    part = own[0].shape[0]
    me = lax.axis_index("mp")
    places = [(own[i], hop, 0) for i, hop in enumerate(order)]
    for end in ends:
        places += [(end.at[pl.ds(i * part, part)], hop, 1) for i, hop in enumerate(order[:len(order) // 2])]
    copies = []
    for i, (piece, hop, flip) in enumerate(places):
        rows = place_of(hop, flip, dense_ref.shape[0], part)
        copies.append(pltpu.make_async_copy(piece, dense_ref.at[rows], sems.at[owners + i]))
        copies[-1].start()
    row = lax.broadcasted_iota(I32, (ROWS_DEV, cap), 0).astype(F32)
    for s in range(owners):
        ids = [pieces[s][cap + q:cap + q + 1, :] for q in range(cap // emb)]
        ids = jnp.concatenate(ids, axis=1)
        hot = jnp.where(row == ids, 1.0, 0.0).astype(BF16)
        wide = pieces[s][:cap, :]
        hi = wide.astype(BF16)
        lo = (wide - hi.astype(F32)).astype(BF16)
        both = jnp.dot(hot, jnp.concatenate([hi, lo], axis=1), preferred_element_type=F32)
        rows_ref[s] = both[:, :emb] + both[:, emb:]
        copy = pltpu.make_async_copy(
            rows_ref.at[s], table_ref.at[peer_from(me, s, owners)], sems.at[s]
        )
        copy.start()
        copies.append(copy)
    for copy in copies:
        copy.wait()


def finish_kernel(order, _, end_ref, dense_ref, sems):
    part = end_ref.shape[0] // len(order)
    copies = []
    for i, hop in enumerate(order):
        rows = place_of(hop, 1, dense_ref.shape[0], part)
        copies.append(pltpu.make_async_copy(end_ref.at[pl.ds(i * part, part)], dense_ref.at[rows], sems.at[i]))
        copies[-1].start()
    for copy in copies:
        copy.wait()


def on_device(pooled, delta, w_first, lookup_slot, row_ids, send_counts):
    owners, n_dp = lax.axis_size("mp"), lax.axis_size("dp")
    examples, emb = pooled.shape
    hid = delta.shape[1]
    width = row_ids.shape[-1]
    cap = width // owners
    slots = lookup_slot[:, 0, :].T
    looks = slots.shape[0]
    counts, ids = send_counts[0], row_ids[0]
    half, part = emb // 2, emb // 8
    tail = -(-cap // (8 * emb)) * 8

    xgrad, delta, pooled, slots, partial = call(
        first_kernel,
        [((emb, examples), F32), (delta.shape, BF16), (pooled.shape, BF16), (slots.shape, I32)]
        + [((2, examples), F32)],
        2 * emb * examples * hid,
        *[pltpu.with_memory_space_constraint(a, pltpu.HBM) for a in (delta, w_first, pooled, slots)],
        specs=[HBM] * 4,
        scratch=[pltpu.VMEM(w_first.shape, BF16), pltpu.SemaphoreType.DMA((3 + examples // CHUNK,))],
    )
    norms = [lax.ppermute(partial, "mp", r) for r in rounds(owners)]
    named, turned, targets, delta_sq = call(
        functools.partial(named_kernel, owners),
        [((width, examples), BF16), ((emb, examples), F32), ((owners, 1, cap), F32)]
        + [((1, examples), F32)],
        8 * width * examples * looks, counts, slots, pooled, ids, delta,
        specs=[SMEM, VMEM, VMEM, VMEM, VMEM],
    )
    clip, scaled, theirs = call(
        clip_kernel,
        [((1, examples), F32), ((half, examples), BF16), ((half, hid), F32)],
        2 * half * examples * hid,
        *norms, partial, turned, delta_sq, delta, named,
        specs=[VMEM] * (len(norms) + 4) + [ANY],
        scratch=[pltpu.VMEM((emb, examples), F32)],
    )
    steps = pairings(owners)
    swap = [(i, i ^ 1) for i in range(n_dp)]
    came = lax.ppermute(theirs, "dp", swap)
    (mine,) = call(mine_kernel, [((half, hid), F32)], 2 * half * examples * hid, scaled, delta)

    def chips(piece, s):
        return lax.ppermute(piece, "dp", [(i, i ^ (2 * s)) for i in range(n_dp)])

    unique = call(
        functools.partial(unique_kernel, owners), [((cap + tail, emb), F32)] * owners,
        4 * width * examples * emb, named, xgrad, clip, targets, mine, specs=[VMEM] * 4 + [ANY],
    )
    hops = (0, 2, 3, 1)
    if n_dp == 8:
        parts = call(
            functools.partial(split_kernel, hops), [((part, hid), F32)] * 4, half * hid, mine, came,
            unique[0], specs=[VMEM, VMEM, ANY],
        )
    else:
        parts = [mine + came]
    for s in range(1, owners):
        unique[s] = lax.ppermute(unique[s], "mp", steps[s - 1])
    if n_dp == 8:
        got = [chips(piece, s) for piece, s in zip(parts[1:], hops[1:])]
        got, unique[0] = lax.optimization_barrier((got, unique[0]))
        total = parts[0] + got[0] + got[1] + got[2]
        order = (0, 3, 1, 2)
        own = [total] + [chips(total, s) for s in order[1:]]
        own[0], *unique = lax.optimization_barrier((own[0], *unique))
        near = jnp.concatenate(own[:2])
        ends = [lax.ppermute(half_of, "dp", swap) for half_of in (near, jnp.concatenate(own[2:]))]
    else:
        groups = [list(range(c, n_dp, 2)) for c in (0, 1)]
        order = (0,)
        own = [lax.psum(parts[0], "dp", axis_index_groups=groups)]
        ends = [lax.ppermute(own[0], "dp", swap)]
    writes = len(own) + len(own) // 2
    table_grad, dense_grad = call(
        functools.partial(place_kernel, owners, cap, order),
        [((owners, ROWS_DEV, emb), F32), ((emb, hid), F32)],
        4 * owners * ROWS_DEV * cap * emb, *unique, *own, *ends[:-1], out_specs=[HBM, HBM],
        scratch=[pltpu.VMEM((owners, ROWS_DEV, emb), F32), pltpu.SemaphoreType.DMA((owners + writes,))],
    )
    rest = order[len(order) // 2:]
    (dense_grad,) = call(
        functools.partial(finish_kernel, rest), [((emb, hid), F32)], 0, dense_grad, ends[-1],
        specs=[HBM, VMEM], out_specs=[HBM], scratch=[pltpu.SemaphoreType.DMA((len(rest),))],
        aliases={0: 0},
    )
    return (dense_grad, table_grad[None])


def solution(mesh):
    placed = (
        P("dp", "mp"),
        P("dp", None),
        P("mp", None),
        P("dp", "mp", None),
        P("dp", "mp", None),
        P("dp", "mp", None),
    )
    return jax.shard_map(
        on_device,
        mesh=mesh,
        in_specs=placed,
        out_specs=(P("mp", None), P("dp", None, "mp", None)),
        check_vma=False,
    )
```
